32 devices in a mesh: groups: 2 (over x), slab: 16 (over z, y, core).
Axes of the slice: x: 2, y: 2, z: 4, core: 2. Of those that a mesh axis runs over, the one named last changes fastest.
Arguments:
- mode_shapes: float32 [16384, 192], P(('groups', 'slab')), parts along dimension 0, may hold values from -6 to 6
- wall_coupling: float32 [16384, 15], P(('groups', 'slab')), parts along dimension 0, may hold values from -3.5 to 3.5
- owner_dev: int32 [16384, 1], P(('groups', 'slab')), parts along dimension 0, may hold values from 0 to 15; in each aligned block of 512 rows (0 to 511, 512 to 1023, ...) at most 64 rows name the same one
- owner_cell: int32 [16384], P(('groups', 'slab')), parts along dimension 0, may hold values from 0 to 2047
- neighbours: int32 [6, 65536], P(None, ('groups', 'slab')), parts along dimension 1, may hold values from -1 to 32767, as said below
- coupling_blocks: float32 [6, 5, 5, 65536], P(None, None, None, ('groups', 'slab')), parts along dimension 3, may hold values from -0.3 to 0.3
- inv_blocks: float32 [5, 5, 65536], P(None, None, ('groups', 'slab')), parts along dimension 2, may hold values from -0.9 to 3, as said below
Outputs:
- modes_basis: float32 [5, 64, 65536], P(None, None, ('groups', 'slab')), parts along dimension 2
- factor: float32 [128, 64], P('groups'), parts along dimension 0
The draws below stay inside these ranges and needn't reach their ends.
There are 2 independent parts, one for each index of `groups`. The reference program is written for one: setup_inputs(seed, part) draws one part's arguments, and reference() takes and returns one part's arrays. A program takes and returns all parts, laid end to end along the dimension named above; each array names one. Nothing has to cross between parts.
Inputs may be any that keep to these rules, and one draw needn't show every extreme that they name: `owner_dev`: in the rows of one slab device at most 64 shell nodes name the same slab, a bound that some of them reach. `neighbours`: A filled slot of cell c names a cell whose number differs from c by 1 to 256. `inv_blocks`: each block has a positive diagonal entry shared by its five diagonal places and off-diagonal entries of at most 0.3 times it in magnitude.
All inputs are finite; a program needn't handle non-finite values.
Results may differ from the reference program's by a relative error of at most 0.0003.
Values sent between devices are 32-bit elements; how exact they have to be, the bound alone decides.
No kernel may reach another device: no remote copies, remote signals or barrier semaphores. Data moves between devices by JAX's collectives and lax.ppermute only.
A program may use at most 192 MiB of HBM per device.

```python
import math
import jax
import jax.numpy as jnp
import numpy as np

VARS = 5
MODES = 64
NBR = 6
SWEEPS = 2
CELL_DEV = 2048
SHELL_DEV = 512
RIM = 256
CAP = 64
CELLS = 32768
SHELL = 8192
N_SLAB = 16


def draw_neighbours(key, part):
    first_key, second_key, third_key = jax.random.split(key, 3)
    numbering = jnp.arange(CELLS, dtype=jnp.int32)
    reach_out = jax.random.randint(first_key, (NBR, CELLS), 1, RIM + 1)
    upward = jax.random.randint(second_key, (NBR, CELLS), 0, 2)
    retained = jax.random.randint(third_key, (NBR, CELLS), 0, 6)
    target = numbering[None, :] + jnp.where(upward == 1, reach_out, -reach_out)
    usable = (target >= 0) & (target < CELLS) & (retained != 0)
    return jnp.where(usable, target, -1).astype(jnp.int32)


def draw_inv_blocks(key, part):
    scale_key, noise_key = jax.random.split(key)
    position = jnp.arange(CELLS, dtype=jnp.float32) / CELLS
    lowest, highest = (0.3, 3.0)
    fraction = jax.random.uniform(scale_key, (CELLS,), jnp.float32)
    scales = jnp.exp(jnp.log(lowest) + fraction * (jnp.log(highest) - jnp.log(lowest)))
    scales = scales * jnp.exp(jnp.log(3.0) * (position - 1.0))
    noise_term = jax.random.uniform(noise_key, (VARS, VARS, CELLS), jnp.float32, -0.3, 0.3)
    identity = jnp.eye(VARS, dtype=jnp.float32)[:, :, None]
    return ((identity + (1.0 - identity) * noise_term) * scales[None, None, :]).astype(jnp.float32)


def set_ends(entries, key, smallest, top_value):
    longest = entries.shape.index(max(entries.shape))
    spots = []
    for shift in (0, 1):
        where = [jax.random.randint(jax.random.fold_in(key, axis), (), 0, length) for axis, length in enumerate(entries.shape)]
        where[longest] = (where[longest] + shift) % entries.shape[longest]
        spots.append(tuple(where))
    return entries.at[spots[0]].set(smallest).at[spots[1]].set(top_value)


def level_of(rng, dims, pieces, least, largest):
    factor_of = 1.0
    for dim, shards_of in pieces:
        draws = jax.random.uniform(jax.random.fold_in(jax.random.fold_in(rng, 6), dim), (shards_of,), jnp.float32, least / len(pieces), largest / len(pieces))
        factor_of = factor_of * jnp.repeat(jnp.exp(draws), dims[dim] // shards_of).reshape((-1,) + (1,) * (len(dims) - 1 - dim))
    return factor_of


def deal_out(key, own, number, rows, amount, top, most, lean):
    sequence = jax.random.permutation(key, amount)
    heavy_load, common = portions_of(amount, rows * top, most, lean, True), portions_of(amount, rows * top, most, lean, False)
    places = jnp.arange(amount)

    def named(sizes, offset_by):
        used = int((sizes > 0).sum())
        fixed = max(1, used // 4)
        moved = fixed + (places - fixed + offset_by * (used - fixed)) % max(1, amount - fixed)
        return jnp.zeros((amount,), jnp.int32).at[sequence[jnp.where(places < fixed, places, moved)]].set(jnp.asarray(sizes, jnp.int32))

    sizes = jnp.where(number % 4 == 0, named(heavy_load, number // 4), named(common, number - number // 4 - 1))
    mixed = jax.random.permutation(jax.random.fold_in(own, 3), amount)
    giver, receiver = mixed[0:amount // 2 * 2:2], mixed[1:amount // 2 * 2:2]
    margin = jnp.minimum(sizes[giver] - 1, most - sizes[receiver]) // 2
    margin = jnp.where((giver == sequence[0]) | (receiver == sequence[0]) | (sizes[receiver] == 0), 0, jnp.maximum(margin, 0))
    moved = jax.random.randint(jax.random.fold_in(own, 4), (amount // 2,), 0, 1 << 20) % (margin + 1)
    sizes = sizes.at[giver].add(-moved).at[receiver].add(moved)
    members = jnp.searchsorted(jnp.cumsum(sizes), jnp.arange(rows * top), side="right").astype(jnp.int32)
    table = members.reshape(top, rows).T
    table = table[jax.random.permutation(jax.random.fold_in(own, 1), rows)]
    offset_by = jax.random.randint(jax.random.fold_in(own, 2), (rows, 1), 0, top)
    return jnp.take_along_axis(table, (jnp.arange(top)[None, :] + offset_by) % top, axis=1)


def portions_of(number_of, total, reach, skew, full):
    portions = [(1 << 20) // math.isqrt(rank ** skew) + 1 for rank in range(1, number_of + 1)]
    largest = reach if full else min(reach, max(-(-total // number_of), total * portions[0] // sum(portions)))
    least = 1 if total - largest >= number_of - 1 else 0
    holding, spare = [largest] + [least] * (number_of - 1), total - largest - least * (number_of - 1)
    while spare > 0:
        free = [i for i in range(1, number_of) if holding[i] < largest] or [i for i in range(1, number_of) if holding[i] < reach]
        whole, left = sum([portions[i] for i in free]), spare
        for i in free:
            extra = min(reach - holding[i], max(1, left * portions[i] // whole), spare)
            holding[i] = holding[i] + extra
            spare = spare - extra
    return np.array(holding)


def scatter_about(rng, dims, deviation, most, pieces=(), kind=jnp.bfloat16):
    array = deviation * jax.random.normal(rng, dims, jnp.float32)
    if pieces:
        array = array * level_of(rng, dims, pieces, -0.22, 0.18)
    return jnp.clip(array, -most, most).astype(kind)


def setup_inputs(seed: int = 0, part: int = 0) -> dict:
    key_of = jax.random.split(jax.random.key(seed), 8)
    part_splits = jax.random.split(jax.random.fold_in(key_of[7], part), 8)
    mode_shapes = scatter_about(part_splits[0], (SHELL, 3 * MODES), 1.0, 6.0, ((0, 16),), jnp.float32)
    wall_coupling = scatter_about(part_splits[1], (SHELL, 3 * VARS), 3 ** -0.5, 3.5, ((0, 16),), jnp.float32)
    owner_dev_keys = jax.random.split(jax.random.fold_in(part_splits[2], 1), SHELL // SHELL_DEV)
    owner_dev_turns = jax.random.permutation(jax.random.fold_in(part_splits[2], 3), SHELL // SHELL_DEV)
    owner_dev = jax.vmap(lambda own, number: deal_out(jax.random.fold_in(part_splits[2], 2), own, number, SHELL_DEV, N_SLAB, 1, CAP, 1))(owner_dev_keys, owner_dev_turns).reshape((SHELL, 1))
    owner_cell = set_ends(jax.random.randint(part_splits[3], (SHELL,), 0, CELL_DEV), jax.random.fold_in(part_splits[3], 1), 0, CELL_DEV - 1).astype(jnp.int32)
    neighbours = draw_neighbours(jax.random.fold_in(jax.random.fold_in(key_of[7], part), 71), part)
    coupling_blocks = scatter_about(part_splits[5], (NBR, VARS, VARS, CELLS), 0.05, 0.3, ((3, 16),), jnp.float32)
    inv_blocks = draw_inv_blocks(jax.random.fold_in(jax.random.fold_in(key_of[7], part), 71), part)
    return dict(mode_shapes=mode_shapes, wall_coupling=wall_coupling, owner_dev=owner_dev, owner_cell=owner_cell, neighbours=neighbours, coupling_blocks=coupling_blocks, inv_blocks=inv_blocks)


def apply_blocks(blocks, field_in):
    rows_out = []
    for out_var in range(field_in.shape[0]):
        summed = blocks[out_var, 0][None, :] * field_in[0]
        for in_var in range(1, field_in.shape[0]):
            summed = summed + blocks[out_var, in_var][None, :] * field_in[in_var]
        rows_out.append(summed)
    return jnp.stack(rows_out)

def couple(weights, shapes):
    node_count = weights.shape[0]
    modes_total = shapes.shape[1] // 3
    weights_split = weights.reshape(node_count, -1, 3)
    shapes_split = shapes.reshape(node_count, 3, modes_total)
    summed = weights_split[:, :, 0, None] * shapes_split[:, None, 0, :]
    for component in range(1, 3):
        summed = summed + weights_split[:, :, component, None] * shapes_split[:, None, component, :]
    return summed.reshape(node_count, -1)

def neighbour_term(field_in, neighbours, coupling_blocks):
    total_cells = field_in.shape[2]
    padded = jnp.concatenate([field_in, jnp.zeros(field_in.shape[:2] + (1,), field_in.dtype)], axis=2)
    safe_ids = jnp.where(neighbours >= 0, neighbours, total_cells).astype(jnp.int32)
    result = jnp.zeros_like(field_in)
    for slot_index in range(NBR):
        gathered = jnp.take(padded, safe_ids[slot_index], axis=2)
        result = result + apply_blocks(coupling_blocks[slot_index], gathered)
    return result

def reference(mode_shapes, wall_coupling, owner_dev, owner_cell, neighbours, coupling_blocks, inv_blocks):
    contribution = couple(wall_coupling, mode_shapes)
    target = (owner_dev[:, 0] * CELL_DEV + owner_cell).astype(jnp.int32)
    forcing = jax.ops.segment_sum(contribution, target, num_segments=CELLS)
    forcing = forcing.T.reshape(VARS, MODES, CELLS)
    state_field = apply_blocks(inv_blocks, forcing)
    for sweep_step in range(SWEEPS):
        state_field = apply_blocks(inv_blocks, forcing - neighbour_term(state_field, neighbours, coupling_blocks))
    matrix = jnp.transpose(state_field, (0, 2, 1)).reshape(VARS * CELLS, MODES)
    basis_out, factor = jnp.linalg.qr(matrix)
    sign_flip = jnp.where(jnp.diagonal(factor) < 0, -1.0, 1.0).astype(factor.dtype)
    basis_out = basis_out * sign_flip[None, :]
    factor = factor * sign_flip[:, None]
    norm_scale = math.sqrt(VARS * CELLS)
    basis_out = jnp.transpose(basis_out.reshape(VARS, CELLS, MODES), (0, 2, 1)) * norm_scale
    return (basis_out, factor / norm_scale)
```

```python
import functools
import math

import jax
import jax.numpy as jnp
from jax import lax
from jax.experimental import pallas as pl
from jax.experimental.pallas import tpu as pltpu
from jax.sharding import PartitionSpec as P

VARS = 5
NBR = 6
BY_LANES = 2
F32, BF16, I32 = jnp.float32, jnp.bfloat16, jnp.int32
VMEM = pl.BlockSpec(memory_space=pltpu.VMEM)


def round_up(value, unit):
    return -(-value // unit) * unit


def split2(x):
    high = x.astype(BF16)
    return high, (x - high.astype(F32)).astype(BF16)


def dot(a, b):
    return jnp.dot(a, b, preferred_element_type=F32)


def call(body, out_shape, *args, name, scratch=(), limit=40, flops=0, **kw):
    return pl.pallas_call(
        body,
        out_shape=out_shape,
        in_specs=kw.pop("in_specs", [VMEM] * len(args)),
        out_specs=kw.pop("out_specs", jax.tree.map(lambda _: VMEM, out_shape)),
        scratch_shapes=list(scratch),
        name=name,
        compiler_params=pltpu.CompilerParams(vmem_limit_bytes=limit << 20),
        **kw,
    )(*args)


def pack_body(cap, groups, rows, shapes_ref, weights_ref, dev_ref, cell_ref, out_ref, rows_ref, lhs_ref):
    nodes, width = shapes_ref.shape
    devices = out_ref.shape[0] // rows
    rows16 = lhs_ref.shape[1] // 3
    used = width + weights_ref.shape[1]
    rows_ref[used - used % 8 :, :] = jnp.zeros((rows_ref.shape[0] - used + used % 8, nodes), F32)
    rows_ref[:width, :] = shapes_ref[...].T
    rows_ref[width:used, :] = weights_ref[...].T
    rows_ref[used : used + 1, :] = (cell_ref[...] + 1).astype(F32)
    for g in range(groups):
        x = rows_ref[g * rows : g * rows + rows16, :]
        high = x.astype(BF16)
        rest = x - high.astype(F32)
        mid = rest.astype(BF16)
        lhs_ref[g, :rows16, :] = high
        lhs_ref[g, rows16 : 2 * rows16, :] = mid
        lhs_ref[g, 2 * rows16 :, :] = (rest - mid.astype(F32)).astype(BF16)
    dest = dev_ref[...]
    named = jnp.where(dest == lax.broadcasted_iota(I32, (nodes, devices), 1), 1.0, 0.0)
    earlier = jnp.where(
        lax.broadcasted_iota(I32, (nodes, nodes), 0) > lax.broadcasted_iota(I32, (nodes, nodes), 1), 1.0, 0.0
    )
    before = dot(earlier.astype(BF16), named.astype(BF16))
    rank = jnp.sum(named * before, axis=1, keepdims=True).astype(I32)
    place = jnp.broadcast_to(dest * 128 + rank, (nodes, 128))
    lane = lax.broadcasted_iota(I32, (nodes, 128), 1)

    def pair(step, _):
        total = jnp.zeros((3 * rows16, 256), F32)
        for g in range(groups):
            hot = [
                jnp.where(place + g * cap == lane + (step * 2 + h) * 128, 1.0, 0.0).astype(BF16) for h in range(2)
            ]
            total = total + dot(lhs_ref[g], jnp.concatenate(hot, axis=1))
        total = total[:rows16] + total[rows16 : 2 * rows16] + total[2 * rows16 :]
        for h in range(2):
            at = pl.multiple_of((step * 2 + h) * rows, 8)
            out_ref[pl.ds(at, rows), :] = total[:rows, h * 128 : (h + 1) * 128]
        return 0

    lax.fori_loop(0, devices // 2, pair, 0)


def prepare_body(rim, near_ref, filled_ref, coupling_ref, inv_ref, blocks_ref, place_ref):
    cells = near_ref.shape[1]
    for j in range(NBR):
        filled = filled_ref[j : j + 1, :] != 0
        for v in range(VARS):
            total = inv_ref[v, 0:1, :] * coupling_ref[j, 0]
            for w in range(1, VARS):
                total = total + inv_ref[v, w : w + 1, :] * coupling_ref[j, w]
            blocks_ref[(j * VARS + v) * 8 : (j * VARS + v) * 8 + VARS, :] = jnp.where(filled, total, 0.0)
        base = lax.broadcasted_iota(I32, (1, cells), 1) // 256 * 256
        place_ref[j : j + 1, :] = jnp.where(filled, near_ref[j : j + 1, :] + rim - base, rim)


def forcing_body(cap, groups, rows, modes, arrived_ref, inv_ref, out_ref, table_ref, lhs_ref, tag_ref):
    devices = arrived_ref.shape[0] // rows
    slots = devices * cap
    cells = out_ref.shape[2]
    lane_group = lax.broadcasted_iota(I32, (rows, 128), 1) // cap
    for p in range(devices // groups):
        chunks = [arrived_ref[(p * groups + b) * rows : (p * groups + b + 1) * rows, :] for b in range(groups)]
        for g in range(groups):
            merged = chunks[g]
            for b in range(groups):
                if b != g:
                    turned = pltpu.roll(chunks[b], (b - g) * cap % 128, 1)
                    merged = jnp.where(lane_group == b, turned, merged)
            table_ref[g * rows : (g + 1) * rows, p * 128 : (p + 1) * 128] = merged
    at = 3 * modes
    tag_row = at + 3 * VARS
    tags = table_ref[tag_row // 8 * 8 : tag_row // 8 * 8 + 8, :].T
    tag_ref[...] = jnp.broadcast_to(tags[:, tag_row % 8 : tag_row % 8 + 1], (slots, 128))
    for v in range(VARS):
        load = table_ref[at + 3 * v : at + 3 * v + 1, :] * table_ref[:modes, :]
        for k in range(1, 3):
            load = load + table_ref[at + 3 * v + k : at + 3 * v + k + 1, :] * table_ref[k * modes : (k + 1) * modes, :]
        high, low = split2(load)
        lhs_ref[v * 2 * modes : v * 2 * modes + modes, :] = high
        lhs_ref[v * 2 * modes + modes : (v + 1) * 2 * modes, :] = low
    lane = lax.broadcasted_iota(I32, (slots, 128), 1) + 1

    def tile(t, _):
        lo = pl.multiple_of(t * 256, 256)
        hot = [jnp.where(tag_ref[...] == (lane + (lo + h * 128)).astype(F32), 1.0, 0.0).astype(BF16) for h in range(2)]
        both = dot(lhs_ref[...], jnp.concatenate(hot, axis=1))
        forcing = [both[u * 2 * modes : u * 2 * modes + modes] + both[u * 2 * modes + modes : (u + 1) * 2 * modes] for u in range(VARS)]
        for v in range(VARS):
            total = inv_ref[v, 0:1, pl.ds(lo, 256)] * forcing[0]
            for u in range(1, VARS):
                total = total + inv_ref[v, u : u + 1, pl.ds(lo, 256)] * forcing[u]
            out_ref[v, :, pl.ds(lo, 256)] = total
        return 0

    lax.fori_loop(0, cells // 256, tile, 0)


def sweep_body(last, x_ref, before_ref, after_ref, start_ref, place_ref, blocks_ref, *refs):
    if last:
        out_ref, gram_ref, ext_ref, two_ref, sum_ref = refs
    else:
        out_ref, ext_ref, two_ref = refs
    modes, cells = x_ref.shape[1:]
    rim = before_ref.shape[2]
    by_matmul = NBR - BY_LANES

    def put(x, u, at):
        ext_ref[u, :, pl.ds(at, 256)] = x
        high, low = split2(x)
        two_ref[u * 2 * modes : u * 2 * modes + modes, pl.ds(at, 256)] = high
        two_ref[u * 2 * modes + modes : (u + 1) * 2 * modes, pl.ds(at, 256)] = low

    for u in range(VARS):
        put(before_ref[u], u, 0)
        put(after_ref[u], u, cells + rim)

    def widen(t, _):
        lo = pl.multiple_of(t * 256, 256)
        for u in range(VARS):
            put(x_ref[u, :, pl.ds(lo, 256)], u, pl.multiple_of(lo + rim, 256))
        return 0

    lax.fori_loop(0, cells // 256, widen, 0)
    if last:
        sum_ref[...] = jnp.zeros_like(sum_ref)
    window = lax.broadcasted_iota(I32, (256 + 2 * rim, 256), 0)

    def tile(t, _):
        lo = pl.multiple_of(t * 256, 256)
        fetched = []
        for j in range(by_matmul):
            hot = jnp.where(window == place_ref[j : j + 1, pl.ds(lo, 256)], 1.0, 0.0).astype(BF16)
            fetched.append(dot(two_ref[:, pl.ds(lo, 256 + 2 * rim)], hot))
        results = [[None] * 2 for _ in range(modes // 8)]
        for m in range(0, modes, 8):
            for h in range(2):
                at = pl.multiple_of(lo + h * 128, 128)
                acc = [start_ref[v, m : m + 8, pl.ds(at, 128)] for v in range(VARS)]

                def subtract(j, u, value):
                    for v in range(VARS):
                        row = (j * VARS + v) * 8 + u
                        acc[v] = acc[v] - blocks_ref[row : row + 1, pl.ds(at, 128)] * value

                around = (128 + 2 * rim) // 128
                source = [[ext_ref[u, m : m + 8, pl.ds(at + s * 128, 128)] for s in range(around)] for u in range(VARS)]
                for j in range(by_matmul, NBR):
                    place = jnp.broadcast_to(place_ref[j : j + 1, pl.ds(at, 128)] - h * 128, (8, 128))
                    lane, block = place & 127, place >> 7
                    for u in range(VARS):
                        value = jnp.take_along_axis(source[u][0], lane, axis=1, mode="promise_in_bounds")
                        for s in range(1, around):
                            there = jnp.take_along_axis(source[u][s], lane, axis=1, mode="promise_in_bounds")
                            value = jnp.where(block == s, there, value)
                        subtract(j, u, value)
                for j in range(by_matmul):
                    for u in range(VARS):
                        r = u * 2 * modes + m
                        both = fetched[j][:, h * 128 : (h + 1) * 128]
                        subtract(j, u, both[r : r + 8] + both[r + modes : r + modes + 8])
                for v in range(VARS):
                    ext_out(v, m, h, at, acc[v])
        if last:
            for v in range(VARS):
                high, low = split2(sum_ref[v, :, :256])
                pair = jnp.concatenate([high, low], axis=0)
                out_ref[v, :, pl.ds(lo, 256)] = pair
                gram_add(pair)
        return 0

    def ext_out(v, m, h, at, value):
        if last:
            sum_ref[v, m : m + 8, h * 128 : (h + 1) * 128] = value
        else:
            out_ref[v, m : m + 8, pl.ds(at, 128)] = value

    def gram_add(pair):
        sum_ref[0, :, 256:384] += lax.dot_general(
            pair[:modes], pair, (((1,), (1,)), ((), ())), preferred_element_type=F32
        )
        sum_ref[1, :, 256:384] += lax.dot_general(
            pair[modes:], pair, (((1,), (1,)), ((), ())), preferred_element_type=F32
        )

    lax.fori_loop(0, cells // 256, tile, 0)
    if last:
        gram = sum_ref[0, :, 256:384] + sum_ref[1, :, 256:384]
        gram = gram + pltpu.roll(gram, modes, 1)
        gram_ref[...] = jnp.where(lax.broadcasted_iota(I32, gram.shape, 1) < modes, gram, 0.0)


def basis_body(norm, gram_ref, field_ref, out_ref, factor_ref, lhs_ref):
    modes = factor_ref.shape[0]

    @pl.when(pl.program_id(0) == 0)
    def _():
        row = lax.broadcasted_iota(I32, (modes, 2 * modes), 0)
        lane = lax.broadcasted_iota(I32, (modes, 2 * modes), 1)
        a = jnp.where(lane == row + modes, 1.0, gram_ref[...])
        for k in range(modes - 1):
            pivot_row = a[k : k + 1, :]
            scale = a[:, k : k + 1] / a[k : k + 1, k : k + 1]
            a = a - jnp.where(row > k, scale, 0.0) * pivot_row
        diagonal = jnp.sum(jnp.where(lane == row, a, 0.0), axis=1, keepdims=True)
        a = a / jnp.sqrt(diagonal)
        factor_ref[...] = jnp.where(lane >= row, a / norm, 0.0)[:, :modes]
        inverse = a * norm
        inverse = jnp.where(lane < modes, pltpu.roll(inverse, modes, 1), inverse)
        high, low = split2(inverse)
        lhs_ref[:modes, :] = high
        lhs_ref[modes:, :] = low

    both = dot(lhs_ref[...], field_ref[0])
    out_ref[0] = both[:modes] + both[modes:]


def local(mode_shapes, wall_coupling, owner_dev, owner_cell, neighbours, coupling_blocks, inv_blocks):
    devices = lax.axis_size("slab")
    cells = inv_blocks.shape[2]
    nodes, modes = mode_shapes.shape[0], mode_shapes.shape[1] // 3
    cap = max(2, 2 * nodes // devices)
    rim = cells // 8
    groups = 128 // cap
    columns = 3 * modes + 3 * VARS + 1
    rows = round_up(-(-columns // groups), 8)
    rows16 = round_up(rows, 16)
    packed = call(
        functools.partial(pack_body, cap, groups, rows),
        jax.ShapeDtypeStruct((devices * rows, 128), F32),
        mode_shapes, wall_coupling, owner_dev, owner_cell[None, :],
        scratch=[pltpu.VMEM(((groups - 1) * rows + rows16, nodes), F32), pltpu.VMEM((groups, 3 * rows16, nodes), BF16)],
        name="pack",
    )
    arrived = lax.all_to_all(packed, "slab", split_axis=0, concat_axis=0, tiled=True)
    near = neighbours - lax.axis_index("slab") * cells
    blocks, place = call(
        functools.partial(prepare_body, rim),
        (jax.ShapeDtypeStruct((NBR * VARS * 8, cells), F32), jax.ShapeDtypeStruct((8, cells), I32)),
        near, (neighbours >= 0).astype(I32), coupling_blocks, inv_blocks,
        name="prepare",
    )
    start = call(
        functools.partial(forcing_body, cap, groups, rows, modes),
        jax.ShapeDtypeStruct((VARS, modes, cells), F32),
        arrived, inv_blocks,
        scratch=[
            pltpu.VMEM((groups * rows, devices * cap), F32),
            pltpu.VMEM((VARS * 2 * modes, devices * cap), BF16),
            pltpu.VMEM((devices * cap, 128), F32),
        ],
        name="forcing",
    )
    up = [(i, i + 1) for i in range(devices - 1)]
    down = [(j, i) for i, j in up]
    x = start
    for last in (False, True):
        before = lax.ppermute(x[:, :, cells - rim :], "slab", up)
        after = lax.ppermute(x[:, :, :rim], "slab", down)
        shapes = jax.ShapeDtypeStruct((VARS, modes, cells), F32)
        scratch = [pltpu.VMEM((VARS, modes, cells + 2 * rim), F32), pltpu.VMEM((VARS * 2 * modes, cells + 2 * rim), BF16)]
        if last:
            shapes = (jax.ShapeDtypeStruct((VARS, 2 * modes, cells), BF16), jax.ShapeDtypeStruct((modes, 2 * modes), F32))
            scratch.append(pltpu.VMEM((VARS, modes, 384), F32))
        x = call(
            functools.partial(sweep_body, last), shapes, x, before, after, start, place, blocks,
            scratch=scratch, name="sweep_last" if last else "sweep",
        )
    field, gram = x
    reach = 1
    while reach < devices:
        gram = gram + lax.ppermute(gram, "slab", [(i, i ^ reach) for i in range(devices)])
        reach *= 2
    norm = math.sqrt(VARS * cells * devices)
    return call(
        functools.partial(basis_body, norm),
        (jax.ShapeDtypeStruct((VARS, modes, cells), F32), jax.ShapeDtypeStruct((modes, modes), F32)),
        gram, field,
        grid=(VARS,),
        in_specs=[
            pl.BlockSpec((modes, 2 * modes), lambda v: (0, 0)),
            pl.BlockSpec((1, 2 * modes, cells), lambda v: (v, 0, 0)),
        ],
        out_specs=(
            pl.BlockSpec((1, modes, cells), lambda v: (v, 0, 0)),
            pl.BlockSpec((modes, modes), lambda v: (0, 0)),
        ),
        scratch=[pltpu.VMEM((2 * modes, 2 * modes), BF16)],
        name="basis",
    )


def solution(mesh):
    in_specs = (
        P(("groups", "slab"), None),
        P(("groups", "slab"), None),
        P(("groups", "slab"), None),
        P(("groups", "slab")),
        P(None, ("groups", "slab")),
        P(None, None, None, ("groups", "slab")),
        P(None, None, ("groups", "slab")),
    )
    out_specs = (P(None, None, ("groups", "slab")), P("groups", None))
    return jax.shard_map(local, mesh=mesh, in_specs=in_specs, out_specs=out_specs, check_vma=False)
```

```python
import functools
import math

import jax
import jax.numpy as jnp
from jax import lax
from jax.experimental import pallas as pl
from jax.experimental.pallas import tpu as pltpu
from jax.sharding import PartitionSpec as P

VARS = 5
NBR = 6
BY_LANES = 2
ROWS = 16
TOGETHER = 4
MANY = 4
STEP = 8
F32, BF16, I32 = jnp.float32, jnp.bfloat16, jnp.int32
VMEM = pl.BlockSpec(memory_space=pltpu.VMEM)


def round_up(value, unit):
    return -(-value // unit) * unit


def split2(x):
    high = x.astype(BF16)
    return high, (x - high.astype(F32)).astype(BF16)


def dot(a, b):
    return jnp.dot(a, b, preferred_element_type=F32)


def call(body, out_shape, *args, name, scratch=(), limit=40, flops=0, **kw):
    return pl.pallas_call(
        body,
        out_shape=out_shape,
        in_specs=kw.pop("in_specs", [VMEM] * len(args)),
        out_specs=kw.pop("out_specs", jax.tree.map(lambda _: VMEM, out_shape)),
        scratch_shapes=list(scratch),
        name=name,
        compiler_params=pltpu.CompilerParams(vmem_limit_bytes=limit << 20),
        **kw,
    )(*args)


def pack_body(cap, groups, rows, shapes_ref, weights_ref, dev_ref, cell_ref, out_ref, rows_ref, lhs_ref):
    width, nodes = shapes_ref.shape
    devices = out_ref.shape[0] // rows
    rows16 = lhs_ref.shape[1] // 3
    used = width + weights_ref.shape[0]
    rows_ref[used - used % 8 :, :] = jnp.zeros((rows_ref.shape[0] - used + used % 8, nodes), F32)
    rows_ref[:width, :] = shapes_ref[...]
    rows_ref[width:used, :] = weights_ref[...]
    rows_ref[used : used + 1, :] = (cell_ref[...] + 1).astype(F32)
    for g in range(groups):
        x = rows_ref[g * rows : g * rows + rows16, :]
        high = x.astype(BF16)
        rest = x - high.astype(F32)
        mid = rest.astype(BF16)
        lhs_ref[g, :rows16, :] = high
        lhs_ref[g, rows16 : 2 * rows16, :] = mid
        lhs_ref[g, 2 * rows16 :, :] = (rest - mid.astype(F32)).astype(BF16)
    dest = dev_ref[...]
    named = jnp.where(dest == lax.broadcasted_iota(I32, (devices, nodes), 0), 1.0, 0.0)
    earlier = jnp.where(
        lax.broadcasted_iota(I32, (nodes, nodes), 0) < lax.broadcasted_iota(I32, (nodes, nodes), 1), 1.0, 0.0
    )
    rank = jnp.sum(named * dot(named.astype(BF16), earlier.astype(BF16)), axis=0, keepdims=True).astype(I32)
    place = dest * 128 + rank
    slot = lax.broadcasted_iota(I32, (128 * MANY, nodes), 0)

    def several(step, _):
        total = jnp.zeros((3 * rows16, 128 * MANY), F32)
        for g in range(groups):
            hot = jnp.where(place + (g * cap - step * 128 * MANY) == slot, 1.0, 0.0).astype(BF16)
            total = total + lax.dot_general(lhs_ref[g], hot, (((1,), (1,)), ((), ())), preferred_element_type=F32)
        total = total[:rows16] + total[rows16 : 2 * rows16] + total[2 * rows16 :]
        for h in range(MANY):
            at = pl.multiple_of((step * MANY + h) * rows, 8)
            out_ref[pl.ds(at, rows), :] = total[:rows, h * 128 : (h + 1) * 128]
        return 0

    lax.fori_loop(0, devices // MANY, several, 0)


def prepare_body(rim, first_ref, neighbours_ref, coupling_ref, inv_ref, blocks_ref, place_ref):
    cells = neighbours_ref.shape[1]
    near = neighbours_ref[...]
    filled = near >= 0
    for u in range(VARS):
        for v in range(VARS):
            total = inv_ref[v, 0:1, :] * coupling_ref[0, u]
            for w in range(1, VARS):
                total = total + inv_ref[v, w : w + 1, :] * coupling_ref[w, u]
            blocks_ref[(v * VARS + u) * 8 : (v * VARS + u) * 8 + NBR, :] = jnp.where(filled, total, 0.0)
    base = lax.broadcasted_iota(I32, (NBR, cells), 1) // 256 * 256 + first_ref[0]
    place_ref[:NBR, :] = jnp.where(filled, near + rim - base, rim)


def forcing_body(cap, groups, rows, modes, rim, arrived_ref, inv_ref, out_ref, two_ref, first_ref, last_ref, table_ref, lhs_ref, tag_ref):
    devices = arrived_ref.shape[0] // rows
    slots = devices * cap
    cells = out_ref.shape[2]
    lane_group = lax.broadcasted_iota(I32, (rows, 128), 1) // cap
    for p in range(devices // groups):
        chunks = [arrived_ref[(p * groups + b) * rows : (p * groups + b + 1) * rows, :] for b in range(groups)]
        for g in range(groups):
            merged = chunks[g]
            for b in range(groups):
                if b != g:
                    turned = pltpu.roll(chunks[b], (b - g) * cap % 128, 1)
                    merged = jnp.where(lane_group == b, turned, merged)
            table_ref[g * rows : (g + 1) * rows, p * 128 : (p + 1) * 128] = merged
    at = 3 * modes
    tag_row = at + 3 * VARS
    tags = table_ref[tag_row // 8 * 8 : tag_row // 8 * 8 + 8, :].T
    tag_ref[...] = jnp.broadcast_to(tags[:, tag_row % 8 : tag_row % 8 + 1], (slots, 128))
    for v in range(VARS):
        load = table_ref[at + 3 * v : at + 3 * v + 1, :] * table_ref[:modes, :]
        for k in range(1, 3):
            load = load + table_ref[at + 3 * v + k : at + 3 * v + k + 1, :] * table_ref[k * modes : (k + 1) * modes, :]
        high, low = split2(load)
        lhs_ref[v * 2 * modes : v * 2 * modes + modes, :] = high
        lhs_ref[v * 2 * modes + modes : (v + 1) * 2 * modes, :] = low
    lane = lax.broadcasted_iota(I32, (slots, 128), 1) + 1

    def tile(t, _):
        lo = pl.multiple_of(t * 512, 512)
        hot = [jnp.where(tag_ref[...] == (lane + (lo + h * 128)).astype(F32), 1.0, 0.0).astype(BF16) for h in range(4)]
        both = dot(lhs_ref[...], jnp.concatenate(hot, axis=1))
        forcing = [both[u * 2 * modes : u * 2 * modes + modes] + both[u * 2 * modes + modes : (u + 1) * 2 * modes] for u in range(VARS)]
        for v in range(VARS):
            total = inv_ref[v, 0:1, pl.ds(lo, 512)] * forcing[0]
            for u in range(1, VARS):
                total = total + inv_ref[v, u : u + 1, pl.ds(lo, 512)] * forcing[u]
            out_ref[v, :, pl.ds(lo, 512)] = total
            high, low = split2(total)
            two_ref[2 * v * modes : (2 * v + 1) * modes, pl.ds(lo, 512)] = high
            two_ref[(2 * v + 1) * modes : (2 * v + 2) * modes, pl.ds(lo, 512)] = low
        return 0

    lax.fori_loop(0, cells // 512, tile, 0)
    first_ref[...] = out_ref[:, :, :rim]
    last_ref[...] = out_ref[:, :, cells - rim :]


def fetch(out_ref, windows, place_ref, lo):
    def step(slots):
        total, at = None, 0
        for two, start, width in windows:
            row = lax.broadcasted_iota(I32, (width, 256), 0) + at
            hot = [jnp.where(row == place_ref[j : j + 1, pl.ds(lo, 256)], 1.0, 0.0).astype(BF16) for j in slots]
            part = dot(two[:, pl.ds(start, width)], jnp.concatenate(hot, axis=1))
            total = part if total is None else total + part
            at += width
        out_ref[:, slots[0] * 256 : (slots[-1] + 1) * 256] = total

    slots = list(range(NBR - BY_LANES))
    return [functools.partial(step, slots[j : j + TOGETHER]) for j in range(0, len(slots), TOGETHER)]


def relax(fetched_ref, source, start_ref, place_ref, blocks_ref, lo, store):
    modes = start_ref.shape[1]
    by_matmul = NBR - BY_LANES
    rows = range(0, ROWS, 8)

    def step(m, h):
        at = pl.multiple_of(lo + h * 128, 128)
        acc = [[start_ref[v, m + i : m + i + 8, pl.ds(at, 128)] for i in rows] for v in range(VARS)]

        def subtract(j, u, values):
            for v in range(VARS):
                row = (v * VARS + u) * 8 + j
                block = blocks_ref[row : row + 1, pl.ds(at, 128)]
                acc[v] = [a - block * value for a, value in zip(acc[v], values)]

        lanes, wheres = [], []
        for j in range(by_matmul, NBR):
            place = jnp.broadcast_to(place_ref[j : j + 1, pl.ds(at, 128)] - h * 128, (8, 128))
            lanes.append(place & 127)
            wheres.append(place >> 7)
        def by_lanes(u):
            around = [[source(u, m + i, h + s) for s in range(5)] for i in rows]
            taken = [
                [[jnp.take_along_axis(x, lane, axis=1, mode="promise_in_bounds") for x in blocks] for blocks in around]
                for lane in lanes
            ]
            for n, where in enumerate(wheres):
                values = []
                for x in taken[n]:
                    value = x[0]
                    for s in range(1, 5):
                        value = jnp.where(where == s, x[s], value)
                    values.append(value)
                subtract(by_matmul + n, u, values)

        def by_dots(u):
            for j in range(by_matmul):
                values = []
                for i in rows:
                    r, c = u * 2 * modes + m + i, j * 256 + h * 128
                    values.append(
                        fetched_ref[r : r + 8, c : c + 128] + fetched_ref[r + modes : r + modes + 8, c : c + 128]
                    )
                subtract(j, u, values)

        for u in range(VARS):
            by_lanes(u)
        for u in range(VARS):
            by_dots(u)
        for v in range(VARS):
            store(v, m, h, jnp.concatenate(acc[v], axis=0))

    return [functools.partial(step, m, h) for m in range(0, modes, ROWS) for h in range(2)]


def run(steps):
    for step in steps:
        step()


def put_two(two_ref, modes, v, m, at, high, low):
    value_rows = high.shape[0]
    two_ref[2 * v * modes + m : 2 * v * modes + m + value_rows, at] = high
    two_ref[(2 * v + 1) * modes + m : (2 * v + 1) * modes + m + value_rows, at] = low


def inner_body(rim, last, x_ref, two_ref, start_ref, place_ref, blocks_ref, *refs):
    if last:
        mid_two_ref, fetched_ref = refs
    else:
        mid_ref, mid_two_ref, fetched_ref = refs
    modes, cells = x_ref.shape[1:]
    tiles = (cells - 2 * rim) // 256

    def load(t, ref):
        lo = pl.multiple_of(rim + t * 256, 256)
        return fetch(ref, [(two_ref, pl.multiple_of(lo - rim, 256), 256 + 2 * rim)], place_ref, lo)

    def work(t, ref):
        lo = pl.multiple_of(rim + t * 256, 256)

        def store(v, m, h, value):
            at = pl.ds(pl.multiple_of(t * 256 + h * 128, 128), 128)
            if not last:
                mid_ref[v, m : m + ROWS, at] = value
            put_two(mid_two_ref, modes, v, m, at, *split2(value))

        def source(u, m, s):
            return x_ref[u, m : m + 8, pl.ds(pl.multiple_of(lo - rim + s * 128, 128), 128)]

        return relax(ref, source, start_ref, place_ref, blocks_ref, lo, store)

    def one_tile(t, _):
        run(load(t, fetched_ref) + work(t, fetched_ref))
        return 0

    lax.fori_loop(0, tiles, one_tile, 0)


def outer_body(rim, last, x_ref, two_ref, before_ref, after_ref, start_ref, place_ref, blocks_ref, *refs):
    if last:
        mid_two_ref, out_two_ref, gram_ref, window_ref, window_two_ref, fetched_ref = refs
    else:
        mid_ref, mid_two_ref, out_ref, out_two_ref, first_ref, last_ref, window_ref, window_two_ref, fetched_ref = refs
    modes, cells = x_ref.shape[1:]
    ends = cells - rim
    near = 256 + rim
    window_ref[0, :, :, :rim] = before_ref[...]
    window_ref[0, :, :, rim:] = x_ref[:, :, :near]
    window_ref[1, :, :, :near] = x_ref[:, :, cells - near :]
    window_ref[1, :, :, near:] = after_ref[...]
    window_two_ref[0, :, rim:] = two_ref[:, :near]
    window_two_ref[1, :, :near] = two_ref[:, cells - near :]
    for side, (ref, at) in enumerate(((before_ref, 0), (after_ref, near))):
        for u in range(VARS):
            high, low = split2(ref[u])
            window_two_ref[side, 2 * u * modes : (2 * u + 1) * modes, at : at + rim] = high
            window_two_ref[side, (2 * u + 1) * modes : (2 * u + 2) * modes, at : at + rim] = low
    out_two_ref[:, rim:ends] = mid_two_ref[...]
    if not last:
        out_ref[:, :, rim:ends] = mid_ref[...]

    def one_side(t, _):
        lo = pl.multiple_of(t * ends, 256)

        def source(u, m, s):
            return window_ref[t, u, m : m + 8, s * 128 : (s + 1) * 128]

        def store(v, m, h, value):
            at = pl.ds(pl.multiple_of(lo + h * 128, 128), 128)
            if not last:
                out_ref[v, m : m + ROWS, at] = value
            put_two(out_two_ref, modes, v, m, at, *split2(value))

        run(
            fetch(fetched_ref, [(window_two_ref.at[t], 0, near + rim)], place_ref, lo)
            + relax(fetched_ref, source, start_ref, place_ref, blocks_ref, lo, store)
        )
        return 0

    lax.fori_loop(0, 2, one_side, 0)
    if not last:
        first_ref[...] = out_ref[:, :, :rim]
        last_ref[...] = out_ref[:, :, ends:]
    if last:
        gram = jnp.zeros((2 * modes, 2 * modes), F32)
        for v in range(VARS):
            both = out_two_ref[2 * v * modes : (2 * v + 2) * modes, :]
            gram = gram + lax.dot_general(both, both, (((1,), (1,)), ((), ())), preferred_element_type=F32)
        gram = gram[:modes] + gram[modes:]
        gram = gram + pltpu.roll(gram, modes, 1)
        gram_ref[...] = jnp.where(lax.broadcasted_iota(I32, gram.shape, 1) < modes, gram, 0.0)


def basis_body(norm, gram_ref, field_ref, out_ref, factor_ref, lhs_ref, inverse_ref):
    modes = factor_ref.shape[0]

    @pl.when(pl.program_id(0) == 0)
    def _():
        row = lax.broadcasted_iota(I32, (8, 2 * modes), 0)
        lane = lax.broadcasted_iota(I32, (8, 2 * modes), 1)
        parts = [jnp.where(lane == row + (i + modes), 1.0, gram_ref[i : i + 8, :]) for i in range(0, modes, 8)]
        pivots = []
        for k in range(0, modes, STEP):
            g, r = k // 8, k % 8
            steps = range(STEP)
            rows = [parts[g][r + i : r + i + 1, :] for i in steps]
            block = [[jnp.broadcast_to(x[:, k + i : k + i + 1], x.shape) for i in steps] for x in rows]
            inverses = []
            for i in steps:
                inverses.append(1.0 / block[i][i])
                for j in range(i + 1, STEP):
                    ratio = block[j][i] * inverses[i]
                    block[j] = [x - ratio * y for x, y in zip(block[j], block[i])]
                    rows[j] = rows[j] - ratio * rows[i]
                pivots.append(block[i][i])
            scaled = [x * inverse for x, inverse in zip(rows, inverses)]
            for n in range(g, modes // 8):
                part = parts[n]
                columns = [jnp.broadcast_to(part[:, k + i : k + i + 1], part.shape) for i in steps]
                for i in steps:
                    for j in range(i + 1, STEP):
                        columns[j] = columns[j] - columns[i] * (block[i][j] * inverses[i])
                for i in steps:
                    column = jnp.where(row >= r + STEP, columns[i], 0.0) if n == g else columns[i]
                    part = part - column * scaled[i]
                if n == g:
                    for i in steps:
                        part = jnp.where(row == r + i, rows[i], part)
                parts[n] = part
        for i in range(modes // 8):
            scale = 1.0 / jnp.sqrt(jnp.concatenate(pivots[i * 8 : (i + 1) * 8], axis=0))
            part = parts[i] * scale
            upper = jnp.where(lane >= row + i * 8, part / norm, 0.0)
            factor_ref[i * 8 : (i + 1) * 8, :] = upper[:, :modes]
            part = part * norm
            inverse_ref[i * 8 : (i + 1) * 8, :] = jnp.where(lane < modes, pltpu.roll(part, modes, 1), part)
        inverse = inverse_ref[...]
        high, low = split2(inverse)
        lhs_ref[:modes, :] = high
        lhs_ref[modes:, :] = low

    both = dot(lhs_ref[...], field_ref[0])
    out_ref[0] = both[:modes] + both[modes:]


def local(mode_shapes, wall_coupling, owner_dev, owner_cell, neighbours, coupling_blocks, inv_blocks):
    devices = lax.axis_size("slab")
    cells = inv_blocks.shape[2]
    nodes, modes = mode_shapes.shape[0], mode_shapes.shape[1] // 3
    cap = max(2, 2 * nodes // devices)
    rim = cells // 8
    groups = 128 // cap
    columns = 3 * modes + 3 * VARS + 1
    rows = round_up(-(-columns // groups), 8)
    rows16 = round_up(rows, 16)
    packed = call(
        functools.partial(pack_body, cap, groups, rows),
        jax.ShapeDtypeStruct((devices * rows, 128), F32),
        mode_shapes.T, wall_coupling.T, owner_dev.T, owner_cell[None, :],
        grid=(1,),
        in_specs=[pl.BlockSpec((n, nodes), lambda i: (0, 0)) for n in (3 * modes, 3 * VARS, 1, 1)],
        out_specs=pl.BlockSpec((devices * rows, 128), lambda i: (0, 0)),
        scratch=[pltpu.VMEM(((groups - 1) * rows + rows16, nodes), F32), pltpu.VMEM((groups, 3 * rows16, nodes), BF16)],
        name="pack", limit=60,
    )
    arrived = lax.all_to_all(packed, "slab", split_axis=0, concat_axis=0, tiled=True)
    field = jax.ShapeDtypeStruct((VARS, modes, cells), F32)
    field_two = jax.ShapeDtypeStruct((VARS * 2 * modes, cells), BF16)
    edge = jax.ShapeDtypeStruct((VARS, modes, rim), F32)
    blocks, place = call(
        functools.partial(prepare_body, rim),
        (jax.ShapeDtypeStruct((VARS * VARS * 8, cells), F32), jax.ShapeDtypeStruct((8, cells), I32)),
        (lax.axis_index("slab") * cells).astype(I32)[None], neighbours, coupling_blocks.transpose(1, 2, 0, 3), inv_blocks,
        in_specs=[pl.BlockSpec(memory_space=pltpu.SMEM)] + [VMEM] * 3,
        cost_estimate=pl.CostEstimate(flops=10**9, bytes_accessed=10**7, transcendentals=0),
        name="prepare",
    )
    start, two, first, final = call(
        functools.partial(forcing_body, cap, groups, rows, modes, rim),
        (field, field_two, edge, edge),
        arrived, inv_blocks,
        scratch=[
            pltpu.VMEM((groups * rows, devices * cap), F32),
            pltpu.VMEM((VARS * 2 * modes, devices * cap), BF16),
            pltpu.VMEM((devices * cap, 128), F32),
        ],
        name="forcing",
    )
    up = [(i, i + 1) for i in range(devices - 1)]
    down = [(j, i) for i, j in up]
    x = start
    inner = cells - 2 * rim
    mid = jax.ShapeDtypeStruct((VARS, modes, inner), F32)
    mid_two = jax.ShapeDtypeStruct((VARS * 2 * modes, inner), BF16)
    fetched = [pltpu.VMEM((VARS * 2 * modes, (NBR - BY_LANES) * 256), F32)]
    cost = pl.CostEstimate(flops=10**10, bytes_accessed=3 * 10**7, transcendentals=0)
    for last in (False, True):
        before = lax.ppermute(final, "slab", up)
        after = lax.ppermute(first, "slab", down)
        middle = call(
            functools.partial(inner_body, rim, last), (mid_two,) if last else (mid, mid_two),
            x, two, start, place, blocks, scratch=fetched, cost_estimate=cost, name="inner_last" if last else "inner",
        )
        windows = [
            pltpu.VMEM((2, VARS, modes, 256 + 2 * rim), F32), pltpu.VMEM((2, VARS * 2 * modes, 256 + 2 * rim), BF16)
        ]
        if last:
            two, gram = call(
                functools.partial(outer_body, rim, last), (field_two, jax.ShapeDtypeStruct((modes, 2 * modes), F32)),
                x, two, before, after, start, place, blocks, *middle,
                scratch=windows + fetched, name="outer_last",
            )
        else:
            x, two, first, final = call(
                functools.partial(outer_body, rim, last), (field, field_two, edge, edge),
                x, two, before, after, start, place, blocks, *middle, scratch=windows + fetched, name="outer",
            )
    field = two.reshape(VARS, 2 * modes, cells)
    reach = 1
    while reach < devices:
        gram = gram + lax.ppermute(gram, "slab", [(i, i ^ reach) for i in range(devices)])
        reach *= 2
    norm = math.sqrt(VARS * cells * devices)
    return call(
        functools.partial(basis_body, norm),
        (jax.ShapeDtypeStruct((VARS, modes, cells), F32), jax.ShapeDtypeStruct((modes, modes), F32)),
        gram, field,
        grid=(VARS,),
        in_specs=[
            pl.BlockSpec((modes, 2 * modes), lambda v: (0, 0)),
            pl.BlockSpec((1, 2 * modes, cells), lambda v: (v, 0, 0)),
        ],
        out_specs=(
            pl.BlockSpec((1, modes, cells), lambda v: (v, 0, 0)),
            pl.BlockSpec((modes, modes), lambda v: (0, 0)),
        ),
        scratch=[pltpu.VMEM((2 * modes, 2 * modes), BF16), pltpu.VMEM((modes, 2 * modes), F32)],
        name="basis",
    )


def solution(mesh):
    in_specs = (
        P(("groups", "slab"), None),
        P(("groups", "slab"), None),
        P(("groups", "slab"), None),
        P(("groups", "slab")),
        P(None, ("groups", "slab")),
        P(None, None, None, ("groups", "slab")),
        P(None, None, ("groups", "slab")),
    )
    out_specs = (P(None, None, ("groups", "slab")), P("groups", None))
    return jax.shard_map(local, mesh=mesh, in_specs=in_specs, out_specs=out_specs, check_vma=False)
```

```python
import functools
import math

import jax
import jax.numpy as jnp
from jax import lax
from jax.experimental import pallas as pl
from jax.experimental.pallas import tpu as pltpu
from jax.sharding import PartitionSpec as P

VARS = 5
NBR = 6
BY_LANES = 2
ROWS = 16
TOGETHER = 4
LIMIT = 16
MANY = 4
STEP = 8
F32, BF16, I32 = jnp.float32, jnp.bfloat16, jnp.int32
VMEM = pl.BlockSpec(memory_space=pltpu.VMEM)


def round_up(value, unit):
    return -(-value // unit) * unit


def split2(x):
    high = x.astype(BF16)
    return high, (x - high.astype(F32)).astype(BF16)


def dot(a, b):
    return jnp.dot(a, b, preferred_element_type=F32)


def call(body, out_shape, *args, name, scratch=(), limit=LIMIT, flops=0, **kw):
    return pl.pallas_call(
        body,
        out_shape=out_shape,
        in_specs=kw.pop("in_specs", [VMEM] * len(args)),
        out_specs=kw.pop("out_specs", jax.tree.map(lambda _: VMEM, out_shape)),
        scratch_shapes=list(scratch),
        name=name,
        compiler_params=pltpu.CompilerParams(vmem_limit_bytes=limit << 20),
        **kw,
    )(*args)


def pack_body(cap, groups, rows, shapes_ref, weights_ref, dev_ref, cell_ref, out_ref, rows_ref, lhs_ref):
    width, nodes = shapes_ref.shape
    devices = out_ref.shape[0] // rows
    rows16 = lhs_ref.shape[1] // 3
    used = width + weights_ref.shape[0]
    rows_ref[used - used % 8 :, :] = jnp.zeros((rows_ref.shape[0] - used + used % 8, nodes), F32)
    rows_ref[:width, :] = shapes_ref[...]
    rows_ref[width:used, :] = weights_ref[...]
    rows_ref[used : used + 1, :] = (cell_ref[...] + 1).astype(F32)
    for g in range(groups):
        x = rows_ref[g * rows : g * rows + rows16, :]
        high = x.astype(BF16)
        rest = x - high.astype(F32)
        mid = rest.astype(BF16)
        lhs_ref[g, :rows16, :] = high
        lhs_ref[g, rows16 : 2 * rows16, :] = mid
        lhs_ref[g, 2 * rows16 :, :] = (rest - mid.astype(F32)).astype(BF16)
    dest = dev_ref[...]
    named = jnp.where(dest == lax.broadcasted_iota(I32, (devices, nodes), 0), 1.0, 0.0)
    earlier = jnp.where(
        lax.broadcasted_iota(I32, (nodes, nodes), 0) < lax.broadcasted_iota(I32, (nodes, nodes), 1), 1.0, 0.0
    )
    rank = jnp.sum(named * dot(named.astype(BF16), earlier.astype(BF16)), axis=0, keepdims=True).astype(I32)
    place = dest * 128 + rank
    slot = lax.broadcasted_iota(I32, (128 * MANY, nodes), 0)

    def several(step, _):
        total = jnp.zeros((3 * rows16, 128 * MANY), F32)
        for g in range(groups):
            hot = jnp.where(place + (g * cap - step * 128 * MANY) == slot, 1.0, 0.0).astype(BF16)
            total = total + lax.dot_general(lhs_ref[g], hot, (((1,), (1,)), ((), ())), preferred_element_type=F32)
        total = total[:rows16] + total[rows16 : 2 * rows16] + total[2 * rows16 :]
        for h in range(MANY):
            at = pl.multiple_of((step * MANY + h) * rows, 8)
            out_ref[pl.ds(at, rows), :] = total[:rows, h * 128 : (h + 1) * 128]
        return 0

    lax.fori_loop(0, devices // MANY, several, 0)


def prepare_body(rim, first_ref, neighbours_ref, coupling_ref, inv_ref, blocks_ref, place_ref):
    cells = neighbours_ref.shape[1]
    near = neighbours_ref[...]
    filled = near >= 0
    for u in range(VARS):
        for v in range(VARS):
            total = inv_ref[v, 0:1, :] * coupling_ref[0, u]
            for w in range(1, VARS):
                total = total + inv_ref[v, w : w + 1, :] * coupling_ref[w, u]
            blocks_ref[(v * VARS + u) * 8 : (v * VARS + u) * 8 + NBR, :] = jnp.where(filled, total, 0.0)
    base = lax.broadcasted_iota(I32, (NBR, cells), 1) // 256 * 256 + first_ref[0]
    place_ref[:NBR, :] = jnp.where(filled, near + rim - base, rim)


def forcing_body(cap, groups, rows, modes, rim, arrived_ref, inv_ref, out_ref, two_ref, first_ref, last_ref, table_ref, lhs_ref, tag_ref):
    devices = arrived_ref.shape[0] // rows
    slots = devices * cap
    cells = out_ref.shape[2]
    lane_group = lax.broadcasted_iota(I32, (rows, 128), 1) // cap
    for p in range(devices // groups):
        chunks = [arrived_ref[(p * groups + b) * rows : (p * groups + b + 1) * rows, :] for b in range(groups)]
        for g in range(groups):
            merged = chunks[g]
            for b in range(groups):
                if b != g:
                    turned = pltpu.roll(chunks[b], (b - g) * cap % 128, 1)
                    merged = jnp.where(lane_group == b, turned, merged)
            table_ref[g * rows : (g + 1) * rows, p * 128 : (p + 1) * 128] = merged
    at = 3 * modes
    tag_row = at + 3 * VARS
    tags = table_ref[tag_row // 8 * 8 : tag_row // 8 * 8 + 8, :].T
    tag_ref[...] = jnp.broadcast_to(tags[:, tag_row % 8 : tag_row % 8 + 1], (slots, 128))
    for v in range(VARS):
        load = table_ref[at + 3 * v : at + 3 * v + 1, :] * table_ref[:modes, :]
        for k in range(1, 3):
            load = load + table_ref[at + 3 * v + k : at + 3 * v + k + 1, :] * table_ref[k * modes : (k + 1) * modes, :]
        high, low = split2(load)
        lhs_ref[v * 2 * modes : v * 2 * modes + modes, :] = high
        lhs_ref[v * 2 * modes + modes : (v + 1) * 2 * modes, :] = low
    lane = lax.broadcasted_iota(I32, (slots, 128), 1) + 1

    def tile(t, _):
        lo = pl.multiple_of(t * 512, 512)
        hot = [jnp.where(tag_ref[...] == (lane + (lo + h * 128)).astype(F32), 1.0, 0.0).astype(BF16) for h in range(4)]
        both = dot(lhs_ref[...], jnp.concatenate(hot, axis=1))
        forcing = [both[u * 2 * modes : u * 2 * modes + modes] + both[u * 2 * modes + modes : (u + 1) * 2 * modes] for u in range(VARS)]
        for v in range(VARS):
            total = inv_ref[v, 0:1, pl.ds(lo, 512)] * forcing[0]
            for u in range(1, VARS):
                total = total + inv_ref[v, u : u + 1, pl.ds(lo, 512)] * forcing[u]
            out_ref[v, :, pl.ds(lo, 512)] = total
            high, low = split2(total)
            two_ref[2 * v * modes : (2 * v + 1) * modes, pl.ds(lo, 512)] = high
            two_ref[(2 * v + 1) * modes : (2 * v + 2) * modes, pl.ds(lo, 512)] = low
        return 0

    lax.fori_loop(0, cells // 512, tile, 0)
    first_ref[...] = out_ref[:, :, :rim]
    last_ref[...] = out_ref[:, :, cells - rim :]


def fetch(out_ref, windows, place_ref, lo):
    def step(slots):
        total, at = None, 0
        for two, start, width in windows:
            row = lax.broadcasted_iota(I32, (width, 256), 0) + at
            hot = [jnp.where(row == place_ref[j : j + 1, pl.ds(lo, 256)], 1.0, 0.0).astype(BF16) for j in slots]
            part = dot(two[:, pl.ds(start, width)], jnp.concatenate(hot, axis=1))
            total = part if total is None else total + part
            at += width
        out_ref[:, slots[0] * 256 : (slots[-1] + 1) * 256] = total

    slots = list(range(NBR - BY_LANES))
    return [functools.partial(step, slots[j : j + TOGETHER]) for j in range(0, len(slots), TOGETHER)]


def relax(fetched_ref, source, start_ref, place_ref, blocks_ref, lo, store):
    modes = start_ref.shape[1]
    by_matmul = NBR - BY_LANES
    rows = range(0, ROWS, 8)

    def step(m, h):
        at = pl.multiple_of(lo + h * 128, 128)
        acc = [[start_ref[v, m + i : m + i + 8, pl.ds(at, 128)] for i in rows] for v in range(VARS)]

        def subtract(j, u, values):
            for v in range(VARS):
                row = (v * VARS + u) * 8 + j
                block = blocks_ref[row : row + 1, pl.ds(at, 128)]
                acc[v] = [a - block * value for a, value in zip(acc[v], values)]

        lanes, wheres = [], []
        for j in range(by_matmul, NBR):
            place = jnp.broadcast_to(place_ref[j : j + 1, pl.ds(at, 128)] - h * 128, (8, 128))
            lanes.append(place & 127)
            wheres.append(place >> 7)
        def by_lanes(u):
            around = [[source(u, m + i, h + s) for s in range(5)] for i in rows]
            taken = [
                [[jnp.take_along_axis(x, lane, axis=1, mode="promise_in_bounds") for x in blocks] for blocks in around]
                for lane in lanes
            ]
            for n, where in enumerate(wheres):
                values = []
                for x in taken[n]:
                    value = x[0]
                    for s in range(1, 5):
                        value = jnp.where(where == s, x[s], value)
                    values.append(value)
                subtract(by_matmul + n, u, values)

        def by_dots(u):
            for j in range(by_matmul):
                values = []
                for i in rows:
                    r, c = u * 2 * modes + m + i, j * 256 + h * 128
                    values.append(
                        fetched_ref[r : r + 8, c : c + 128] + fetched_ref[r + modes : r + modes + 8, c : c + 128]
                    )
                subtract(j, u, values)

        for u in range(VARS):
            by_lanes(u)
        for u in range(VARS):
            by_dots(u)
        for v in range(VARS):
            store(v, m, h, jnp.concatenate(acc[v], axis=0))

    return [functools.partial(step, m, h) for m in range(0, modes, ROWS) for h in range(2)]


def run(steps):
    for step in steps:
        step()


def put_two(two_ref, modes, v, m, at, high, low):
    value_rows = high.shape[0]
    two_ref[2 * v * modes + m : 2 * v * modes + m + value_rows, at] = high
    two_ref[(2 * v + 1) * modes + m : (2 * v + 1) * modes + m + value_rows, at] = low


def inner_body(rim, last, x_ref, two_ref, start_ref, place_ref, blocks_ref, *refs):
    if last:
        mid_two_ref, fetched_ref = refs
    else:
        mid_ref, mid_two_ref, fetched_ref = refs
    modes, cells = x_ref.shape[1:]
    tiles = (cells - 2 * rim) // 256

    def load(t, ref):
        lo = pl.multiple_of(rim + t * 256, 256)
        return fetch(ref, [(two_ref, pl.multiple_of(lo - rim, 256), 256 + 2 * rim)], place_ref, lo)

    def work(t, ref):
        lo = pl.multiple_of(rim + t * 256, 256)

        def store(v, m, h, value):
            at = pl.ds(pl.multiple_of(t * 256 + h * 128, 128), 128)
            if not last:
                mid_ref[v, m : m + ROWS, at] = value
            put_two(mid_two_ref, modes, v, m, at, *split2(value))

        def source(u, m, s):
            return x_ref[u, m : m + 8, pl.ds(pl.multiple_of(lo - rim + s * 128, 128), 128)]

        return relax(ref, source, start_ref, place_ref, blocks_ref, lo, store)

    def one_tile(t, _):
        run(load(t, fetched_ref) + work(t, fetched_ref))
        return 0

    lax.fori_loop(0, tiles, one_tile, 0)


def outer_body(rim, last, x_ref, two_ref, before_ref, after_ref, start_ref, place_ref, blocks_ref, *refs):
    if last:
        mid_two_ref, out_two_ref, gram_ref, window_ref, window_two_ref, fetched_ref = refs
    else:
        mid_ref, mid_two_ref, out_ref, out_two_ref, first_ref, last_ref, window_ref, window_two_ref, fetched_ref = refs
    modes, cells = x_ref.shape[1:]
    ends = cells - rim
    near = 256 + rim
    window_ref[0, :, :, :rim] = before_ref[...]
    window_ref[0, :, :, rim:] = x_ref[:, :, :near]
    window_ref[1, :, :, :near] = x_ref[:, :, cells - near :]
    window_ref[1, :, :, near:] = after_ref[...]
    window_two_ref[0, :, rim:] = two_ref[:, :near]
    window_two_ref[1, :, :near] = two_ref[:, cells - near :]
    for side, (ref, at) in enumerate(((before_ref, 0), (after_ref, near))):
        for u in range(VARS):
            high, low = split2(ref[u])
            window_two_ref[side, 2 * u * modes : (2 * u + 1) * modes, at : at + rim] = high
            window_two_ref[side, (2 * u + 1) * modes : (2 * u + 2) * modes, at : at + rim] = low
    out_two_ref[:, rim:ends] = mid_two_ref[...]
    if not last:
        out_ref[:, :, rim:ends] = mid_ref[...]

    def one_side(t, _):
        lo = pl.multiple_of(t * ends, 256)

        def source(u, m, s):
            return window_ref[t, u, m : m + 8, s * 128 : (s + 1) * 128]

        def store(v, m, h, value):
            at = pl.ds(pl.multiple_of(lo + h * 128, 128), 128)
            if not last:
                out_ref[v, m : m + ROWS, at] = value
            put_two(out_two_ref, modes, v, m, at, *split2(value))

        run(
            fetch(fetched_ref, [(window_two_ref.at[t], 0, near + rim)], place_ref, lo)
            + relax(fetched_ref, source, start_ref, place_ref, blocks_ref, lo, store)
        )
        return 0

    lax.fori_loop(0, 2, one_side, 0)
    if not last:
        first_ref[...] = out_ref[:, :, :rim]
        last_ref[...] = out_ref[:, :, ends:]
    if last:
        gram = jnp.zeros((2 * modes, 2 * modes), F32)
        for v in range(VARS):
            both = out_two_ref[2 * v * modes : (2 * v + 2) * modes, :]
            gram = gram + lax.dot_general(both, both, (((1,), (1,)), ((), ())), preferred_element_type=F32)
        gram = gram[:modes] + gram[modes:]
        gram = gram + pltpu.roll(gram, modes, 1)
        half = modes // 2
        gram_ref[...] = jnp.where(lax.broadcasted_iota(I32, (half, 2 * modes), 1) < modes, gram[:half], gram[half:])


def basis_body(norm, gram_ref, field_ref, out_ref, factor_ref, inverse_ref, held_ref, done_ref):
    modes = factor_ref.shape[0]
    row = lax.broadcasted_iota(I32, (8, 2 * modes), 0)
    lane = lax.broadcasted_iota(I32, (8, 2 * modes), 1)
    parts = []
    for i in range(0, modes, 8):
        x = gram_ref[i % (modes // 2) : i % (modes // 2) + 8, :]
        x = x if i < modes // 2 else pltpu.roll(x, modes, 1)
        parts.append(jnp.where(lane < modes, x, jnp.where(lane == row + (i + modes), 1.0, 0.0)))
    pivots = []
    for k in range(0, modes, STEP):
        g, r = k // 8, k % 8
        steps = range(STEP)
        rows = [parts[g][r + i : r + i + 1, :] for i in steps]
        block = [[jnp.broadcast_to(x[:, k + i : k + i + 1], x.shape) for i in steps] for x in rows]
        inverses = []
        for i in steps:
            inverses.append(1.0 / block[i][i])
            for j in range(i + 1, STEP):
                ratio = block[j][i] * inverses[i]
                block[j] = [x - ratio * y for x, y in zip(block[j], block[i])]
                rows[j] = rows[j] - ratio * rows[i]
            pivots.append(block[i][i])
        scaled = [x * inverse for x, inverse in zip(rows, inverses)]
        for n in range(g, modes // 8):
            part = parts[n]
            columns = [jnp.broadcast_to(part[:, k + i : k + i + 1], part.shape) for i in steps]
            for i in steps:
                for j in range(i + 1, STEP):
                    columns[j] = columns[j] - columns[i] * (block[i][j] * inverses[i])
            for i in steps:
                column = jnp.where(row >= r + STEP, columns[i], 0.0) if n == g else columns[i]
                part = part - column * scaled[i]
            if n == g:
                for i in steps:
                    part = jnp.where(row == r + i, rows[i], part)
            parts[n] = part
    for i in range(modes // 8):
        scale = 1.0 / jnp.sqrt(jnp.concatenate(pivots[i * 8 : (i + 1) * 8], axis=0))
        part = parts[i] * scale
        upper = jnp.where(lane >= row + i * 8, part / norm, 0.0)
        factor_ref[i * 8 : (i + 1) * 8, :] = upper[:, :modes]
        part = part * norm
        inverse_ref[i * 8 : (i + 1) * 8, :] = jnp.where(lane < modes, pltpu.roll(part, modes, 1), part)
    lhs = jnp.concatenate(split2(inverse_ref[...]), axis=0)
    copies = []
    for v in range(VARS):
        both = dot(lhs, field_ref[2 * v * modes : (2 * v + 2) * modes, :])
        held_ref[v] = both[:modes] + both[modes:]
        copies.append(pltpu.make_async_copy(held_ref.at[v], out_ref.at[v], done_ref.at[v]))
        copies[-1].start()
    for copy in copies:
        copy.wait()


def local(mode_shapes, wall_coupling, owner_dev, owner_cell, neighbours, coupling_blocks, inv_blocks):
    devices = lax.axis_size("slab")
    cells = inv_blocks.shape[2]
    nodes, modes = mode_shapes.shape[0], mode_shapes.shape[1] // 3
    cap = max(2, 2 * nodes // devices)
    rim = cells // 8
    groups = 128 // cap
    columns = 3 * modes + 3 * VARS + 1
    rows = round_up(-(-columns // groups), 8)
    rows16 = round_up(rows, 16)
    packed = call(
        functools.partial(pack_body, cap, groups, rows),
        jax.ShapeDtypeStruct((devices * rows, 128), F32),
        mode_shapes.T, wall_coupling.T, owner_dev.T, owner_cell[None, :],
        grid=(1,),
        in_specs=[pl.BlockSpec((n, nodes), lambda i: (0, 0)) for n in (3 * modes, 3 * VARS, 1, 1)],
        out_specs=pl.BlockSpec((devices * rows, 128), lambda i: (0, 0)),
        scratch=[pltpu.VMEM(((groups - 1) * rows + rows16, nodes), F32), pltpu.VMEM((groups, 3 * rows16, nodes), BF16)],
        name="pack", limit=60,
    )
    arrived = lax.all_to_all(packed, "slab", split_axis=0, concat_axis=0, tiled=True)
    field = jax.ShapeDtypeStruct((VARS, modes, cells), F32)
    field_two = jax.ShapeDtypeStruct((VARS * 2 * modes, cells), BF16)
    edge = jax.ShapeDtypeStruct((VARS, modes, rim), F32)
    blocks, place = call(
        functools.partial(prepare_body, rim),
        (jax.ShapeDtypeStruct((VARS * VARS * 8, cells), F32), jax.ShapeDtypeStruct((8, cells), I32)),
        (lax.axis_index("slab") * cells).astype(I32)[None], neighbours, coupling_blocks.transpose(1, 2, 0, 3), inv_blocks,
        in_specs=[pl.BlockSpec(memory_space=pltpu.SMEM)] + [VMEM] * 3,
        cost_estimate=pl.CostEstimate(flops=10**9, bytes_accessed=10**7, transcendentals=0),
        name="prepare",
    )
    start, two, first, final = call(
        functools.partial(forcing_body, cap, groups, rows, modes, rim),
        (field, field_two, edge, edge),
        arrived, inv_blocks,
        scratch=[
            pltpu.VMEM((groups * rows, devices * cap), F32),
            pltpu.VMEM((VARS * 2 * modes, devices * cap), BF16),
            pltpu.VMEM((devices * cap, 128), F32),
        ],
        name="forcing",
    )
    up = [(i, i + 1) for i in range(devices - 1)]
    down = [(j, i) for i, j in up]
    x = start
    inner = cells - 2 * rim
    mid = jax.ShapeDtypeStruct((VARS, modes, inner), F32)
    mid_two = jax.ShapeDtypeStruct((VARS * 2 * modes, inner), BF16)
    fetched = [pltpu.VMEM((VARS * 2 * modes, (NBR - BY_LANES) * 256), F32)]
    cost = pl.CostEstimate(flops=10**10, bytes_accessed=3 * 10**7, transcendentals=0)
    for last in (False, True):
        before = lax.ppermute(final, "slab", up)
        after = lax.ppermute(first, "slab", down)
        middle = call(
            functools.partial(inner_body, rim, last), (mid_two,) if last else (mid, mid_two),
            x, two, start, place, blocks, scratch=fetched, cost_estimate=cost, name="inner_last" if last else "inner",
        )
        windows = [
            pltpu.VMEM((2, VARS, modes, 256 + 2 * rim), F32), pltpu.VMEM((2, VARS * 2 * modes, 256 + 2 * rim), BF16)
        ]
        if last:
            two, gram = call(
                functools.partial(outer_body, rim, last), (field_two, jax.ShapeDtypeStruct((modes // 2, 2 * modes), F32)),
                x, two, before, after, start, place, blocks, *middle,
                scratch=windows + fetched, name="outer_last",
            )
        else:
            x, two, first, final = call(
                functools.partial(outer_body, rim, last), (field, field_two, edge, edge),
                x, two, before, after, start, place, blocks, *middle, scratch=windows + fetched, name="outer",
            )
    reach = 1
    while reach < devices:
        gram = gram + lax.ppermute(gram, "slab", [(i, i ^ reach) for i in range(devices)])
        reach *= 2
    norm = math.sqrt(VARS * cells * devices)
    return call(
        functools.partial(basis_body, norm),
        (jax.ShapeDtypeStruct((VARS, modes, cells), F32), jax.ShapeDtypeStruct((modes, modes), F32)),
        gram, two,
        out_specs=(pl.BlockSpec(memory_space=pl.ANY), VMEM),
        scratch=[
            pltpu.VMEM((modes, 2 * modes), F32), pltpu.VMEM((VARS, modes, cells), F32), pltpu.SemaphoreType.DMA((VARS,))
        ],
        name="basis",
    )


def solution(mesh):
    in_specs = (
        P(("groups", "slab"), None),
        P(("groups", "slab"), None),
        P(("groups", "slab"), None),
        P(("groups", "slab")),
        P(None, ("groups", "slab")),
        P(None, None, None, ("groups", "slab")),
        P(None, None, ("groups", "slab")),
    )
    out_specs = (P(None, None, ("groups", "slab")), P("groups", None))
    return jax.shard_map(local, mesh=mesh, in_specs=in_specs, out_specs=out_specs, check_vma=False)
```

```python
import functools
import math

import jax
import jax.numpy as jnp
from jax import lax
from jax.experimental import pallas as pl
from jax.experimental.pallas import tpu as pltpu
from jax.sharding import PartitionSpec as P

VARS = 5
NBR = 6
BY_LANES = 2
ROWS = 32
ORDER = (("F", 0), ("L", 0), ("F", 1), ("L", 1), ("D", 0), ("D", 1))
LIMIT = 16
MANY = 4
STEP = 8
F32, BF16, I32 = jnp.float32, jnp.bfloat16, jnp.int32
VMEM = pl.BlockSpec(memory_space=pltpu.VMEM)


def round_up(value, unit):
    return -(-value // unit) * unit


def split2(x):
    high = x.astype(BF16)
    return high, (x - high.astype(F32)).astype(BF16)


def dot(a, b):
    return jnp.dot(a, b, preferred_element_type=F32)


def call(body, out_shape, *args, name, scratch=(), limit=LIMIT, flops=0, **kw):
    return pl.pallas_call(
        body,
        out_shape=out_shape,
        in_specs=kw.pop("in_specs", [VMEM] * len(args)),
        out_specs=kw.pop("out_specs", jax.tree.map(lambda _: VMEM, out_shape)),
        scratch_shapes=list(scratch),
        name=name,
        compiler_params=pltpu.CompilerParams(vmem_limit_bytes=limit << 20),
        **kw,
    )(*args)


def pack_body(cap, groups, rows, shapes_ref, weights_ref, dev_ref, cell_ref, out_ref, rows_ref, lhs_ref):
    width, nodes = shapes_ref.shape
    devices = out_ref.shape[0] // rows
    rows16 = lhs_ref.shape[1] // 2
    used = width + weights_ref.shape[0]
    rows_ref[used - used % 8 :, :] = jnp.zeros((rows_ref.shape[0] - used + used % 8, nodes), F32)
    rows_ref[:width, :] = shapes_ref[...]
    rows_ref[width:used, :] = weights_ref[...]
    rows_ref[used : used + 1, :] = (cell_ref[...] + 1).astype(F32)
    for g in range(groups):
        x = rows_ref[g * rows : g * rows + rows16, :]
        lhs_ref[g, :rows16, :], lhs_ref[g, rows16:, :] = split2(x)
    dest = dev_ref[...]
    named = jnp.where(dest == lax.broadcasted_iota(I32, (devices, nodes), 0), 1.0, 0.0)
    earlier = jnp.where(
        lax.broadcasted_iota(I32, (nodes, nodes), 0) < lax.broadcasted_iota(I32, (nodes, nodes), 1), 1.0, 0.0
    )
    rank = jnp.sum(named * dot(named.astype(BF16), earlier.astype(BF16)), axis=0, keepdims=True).astype(I32)
    place = dest * 128 + rank
    slot = lax.broadcasted_iota(I32, (128 * MANY, nodes), 0)

    def several(step, _):
        total = jnp.zeros((2 * rows16, 128 * MANY), F32)
        for g in range(groups):
            hot = jnp.where(place + (g * cap - step * 128 * MANY) == slot, 1.0, 0.0).astype(BF16)
            total = total + lax.dot_general(lhs_ref[g], hot, (((1,), (1,)), ((), ())), preferred_element_type=F32)
        total = total[:rows16] + total[rows16:]
        for h in range(MANY):
            at = pl.multiple_of((step * MANY + h) * rows, 8)
            out_ref[pl.ds(at, rows), :] = total[:rows, h * 128 : (h + 1) * 128]
        return 0

    lax.fori_loop(0, devices // MANY, several, 0)


def prepare_body(rim, first_ref, neighbours_ref, coupling_ref, inv_ref, blocks_ref, place_ref):
    cells = neighbours_ref.shape[1]
    near = neighbours_ref[...]
    filled = near >= 0
    for u in range(VARS):
        for v in range(VARS):
            total = inv_ref[v, 0:1, :] * coupling_ref[0, u]
            for w in range(1, VARS):
                total = total + inv_ref[v, w : w + 1, :] * coupling_ref[w, u]
            blocks_ref[(v * VARS + u) * 8 : (v * VARS + u) * 8 + NBR, :] = jnp.where(filled, total, 0.0)
    base = lax.broadcasted_iota(I32, (NBR, cells), 1) // 256 * 256 + first_ref[0]
    place_ref[:NBR, :] = jnp.where(filled, near + rim - base, rim)


def forcing_body(cap, groups, rows, modes, rim, arrived_ref, inv_ref, out_ref, two_ref, first_ref, last_ref, table_ref, lhs_ref, tag_ref):
    devices = arrived_ref.shape[0] // rows
    slots = devices * cap
    cells = out_ref.shape[2]
    lane_group = lax.broadcasted_iota(I32, (rows, 128), 1) // cap
    for p in range(devices // groups):
        chunks = [arrived_ref[(p * groups + b) * rows : (p * groups + b + 1) * rows, :] for b in range(groups)]
        for g in range(groups):
            merged = chunks[g]
            for b in range(groups):
                if b != g:
                    turned = pltpu.roll(chunks[b], (b - g) * cap % 128, 1)
                    merged = jnp.where(lane_group == b, turned, merged)
            table_ref[g * rows : (g + 1) * rows, p * 128 : (p + 1) * 128] = merged
    at = 3 * modes
    tag_row = at + 3 * VARS
    tags = table_ref[tag_row // 8 * 8 : tag_row // 8 * 8 + 8, :].T
    tag_ref[...] = jnp.broadcast_to(tags[:, tag_row % 8 : tag_row % 8 + 1], (slots, 128))
    for v in range(VARS):
        load = table_ref[at + 3 * v : at + 3 * v + 1, :] * table_ref[:modes, :]
        for k in range(1, 3):
            load = load + table_ref[at + 3 * v + k : at + 3 * v + k + 1, :] * table_ref[k * modes : (k + 1) * modes, :]
        high, low = split2(load)
        lhs_ref[v * 2 * modes : v * 2 * modes + modes, :] = high
        lhs_ref[v * 2 * modes + modes : (v + 1) * 2 * modes, :] = low
    lane = lax.broadcasted_iota(I32, (slots, 128), 1) + 1

    def tile(t, _):
        lo = pl.multiple_of(t * 1024, 1024)
        hot = [jnp.where(tag_ref[...] == (lane + (lo + h * 128)).astype(F32), 1.0, 0.0).astype(BF16) for h in range(8)]
        both = dot(lhs_ref[...], jnp.concatenate(hot, axis=1))
        forcing = [both[u * 2 * modes : u * 2 * modes + modes] + both[u * 2 * modes + modes : (u + 1) * 2 * modes] for u in range(VARS)]
        for v in range(VARS):
            total = inv_ref[v, 0:1, pl.ds(lo, 1024)] * forcing[0]
            for u in range(1, VARS):
                total = total + inv_ref[v, u : u + 1, pl.ds(lo, 1024)] * forcing[u]
            out_ref[v, :, pl.ds(lo, 1024)] = total
            high, low = split2(total)
            two_ref[2 * v * modes : (2 * v + 1) * modes, pl.ds(lo, 1024)] = high
            two_ref[(2 * v + 1) * modes : (2 * v + 2) * modes, pl.ds(lo, 1024)] = low
        return 0

    lax.fori_loop(0, cells // 1024, tile, 0)
    first_ref[...] = out_ref[:, :, :rim]
    last_ref[...] = out_ref[:, :, cells - rim :]


def relax(fetched_ref, part_ref, two, source, start_ref, place_ref, blocks_ref, lo, store):
    modes = start_ref.shape[1]
    by_matmul = NBR - BY_LANES
    rows = range(0, ROWS, 8)
    two_ref, first = two

    def subtract(acc, at, j, u, values):
        for v in range(VARS):
            row = (v * VARS + u) * 8 + j
            block = blocks_ref[row : row + 1, pl.ds(at, 128)]
            acc[v] = [a - block * value for a, value in zip(acc[v], values)]

    def fetch(h):
        at = pl.multiple_of(lo + h * 128, 128)
        row = lax.broadcasted_iota(I32, (640, 128), 0) + h * 128
        hot = [jnp.where(row == place_ref[j : j + 1, pl.ds(at, 128)], 1.0, 0.0).astype(BF16) for j in range(by_matmul)]
        window = pl.ds(pl.multiple_of(first + h * 128, 128), 640)
        fetched_ref[:, h * by_matmul * 128 : (h + 1) * by_matmul * 128] = dot(two_ref[:, window], jnp.concatenate(hot, axis=1))

    def lanes(h):
        at = pl.multiple_of(lo + h * 128, 128)
        picks = []
        for j in range(by_matmul, NBR):
            place = jnp.broadcast_to(place_ref[j : j + 1, pl.ds(at, 128)] - h * 128, (8, 128))
            picks.append((j, place & 127, place >> 7))
        for m in range(0, modes, ROWS):
            acc = [[start_ref[v, m + i : m + i + 8, pl.ds(at, 128)] for i in rows] for v in range(VARS)]
            for u in range(VARS):
                around = [[source(u, m + i, h + s) for s in range(5)] for i in rows]
                taken = [
                    [[jnp.take_along_axis(x, lane, axis=1, mode="promise_in_bounds") for x in blocks] for blocks in around]
                    for _, lane, _ in picks
                ]
                for (j, _, where), found in zip(picks, taken):
                    values = []
                    for x in found:
                        value = x[0]
                        for s in range(1, 5):
                            value = jnp.where(where == s, x[s], value)
                        values.append(value)
                    subtract(acc, at, j, u, values)
            for v in range(VARS):
                for n, i in enumerate(rows):
                    part_ref[h, v, m + i : m + i + 8, :] = acc[v][n]

    def dots(h):
        at = pl.multiple_of(lo + h * 128, 128)
        for m in range(0, modes, ROWS):
            acc = [[part_ref[h, v, m + i : m + i + 8, :] for i in rows] for v in range(VARS)]
            for u in range(VARS):
                for j in range(by_matmul):
                    values = []
                    for i in rows:
                        r, c = u * 2 * modes + m + i, (h * by_matmul + j) * 128
                        values.append(
                            fetched_ref[r : r + 8, c : c + 128] + fetched_ref[r + modes : r + modes + 8, c : c + 128]
                        )
                    subtract(acc, at, j, u, values)
            for v in range(VARS):
                store(v, m, h, jnp.concatenate(acc[v], axis=0))

    for step, h in ORDER:
        {"F": fetch, "L": lanes, "D": dots}[step](h)


def put_two(two_ref, modes, v, m, at, high, low):
    value_rows = high.shape[0]
    two_ref[2 * v * modes + m : 2 * v * modes + m + value_rows, at] = high
    two_ref[(2 * v + 1) * modes + m : (2 * v + 1) * modes + m + value_rows, at] = low


def inner_body(rim, last, x_ref, two_ref, start_ref, place_ref, blocks_ref, *refs):
    if last:
        mid_two_ref, fetched_ref, part_ref = refs
    else:
        mid_ref, mid_two_ref, fetched_ref, part_ref = refs
    modes, cells = x_ref.shape[1:]
    tiles = (cells - 2 * rim) // 256

    def one_tile(t, _):
        lo = pl.multiple_of(rim + t * 256, 256)

        def store(v, m, h, value):
            at = pl.ds(pl.multiple_of(t * 256 + h * 128, 128), 128)
            if not last:
                mid_ref[v, m : m + ROWS, at] = value
            put_two(mid_two_ref, modes, v, m, at, *split2(value))

        def source(u, m, s):
            return x_ref[u, m : m + 8, pl.ds(pl.multiple_of(lo - rim + s * 128, 128), 128)]

        two = (two_ref, pl.multiple_of(lo - rim, 256))
        relax(fetched_ref, part_ref, two, source, start_ref, place_ref, blocks_ref, lo, store)
        return 0

    lax.fori_loop(0, tiles, one_tile, 0)


def outer_body(rim, last, x_ref, two_ref, before_ref, after_ref, start_ref, place_ref, blocks_ref, *refs):
    if last:
        mid_two_ref, out_two_ref, gram_ref, window_ref, window_two_ref, fetched_ref, part_ref = refs
    else:
        mid_ref, mid_two_ref, out_ref, out_two_ref, first_ref, last_ref, window_ref, window_two_ref, fetched_ref, part_ref = refs
    modes, cells = x_ref.shape[1:]
    ends = cells - rim
    near = 256 + rim
    window_ref[0, :, :, :rim] = before_ref[...]
    window_ref[0, :, :, rim:] = x_ref[:, :, :near]
    window_ref[1, :, :, :near] = x_ref[:, :, cells - near :]
    window_ref[1, :, :, near:] = after_ref[...]
    window_two_ref[0, :, rim:] = two_ref[:, :near]
    window_two_ref[1, :, :near] = two_ref[:, cells - near :]
    for side, (ref, at) in enumerate(((before_ref, 0), (after_ref, near))):
        for u in range(VARS):
            high, low = split2(ref[u])
            window_two_ref[side, 2 * u * modes : (2 * u + 1) * modes, at : at + rim] = high
            window_two_ref[side, (2 * u + 1) * modes : (2 * u + 2) * modes, at : at + rim] = low
    out_two_ref[:, rim:ends] = mid_two_ref[...]
    if not last:
        out_ref[:, :, rim:ends] = mid_ref[...]

    def one_side(t, _):
        lo = pl.multiple_of(t * ends, 256)

        def source(u, m, s):
            return window_ref[t, u, m : m + 8, s * 128 : (s + 1) * 128]

        def store(v, m, h, value):
            at = pl.ds(pl.multiple_of(lo + h * 128, 128), 128)
            if not last:
                out_ref[v, m : m + ROWS, at] = value
            put_two(out_two_ref, modes, v, m, at, *split2(value))

        two = (window_two_ref.at[t], 0)
        relax(fetched_ref, part_ref, two, source, start_ref, place_ref, blocks_ref, lo, store)
        return 0

    lax.fori_loop(0, 2, one_side, 0)
    if not last:
        first_ref[...] = out_ref[:, :, :rim]
        last_ref[...] = out_ref[:, :, ends:]
    if last:
        gram = jnp.zeros((2 * modes, 2 * modes), F32)
        for v in range(VARS):
            both = out_two_ref[2 * v * modes : (2 * v + 2) * modes, :]
            gram = gram + lax.dot_general(both, both, (((1,), (1,)), ((), ())), preferred_element_type=F32)
        gram = gram[:modes] + gram[modes:]
        gram = gram + pltpu.roll(gram, modes, 1)
        half = modes // 2
        gram_ref[...] = jnp.where(lax.broadcasted_iota(I32, (half, 2 * modes), 1) < modes, gram[:half], gram[half:])


def basis_body(norm, gram_ref, field_ref, out_ref, factor_ref, inverse_ref, held_ref, done_ref):
    modes = factor_ref.shape[0]
    row = lax.broadcasted_iota(I32, (8, 2 * modes), 0)
    lane = lax.broadcasted_iota(I32, (8, 2 * modes), 1)
    parts = []
    for i in range(0, modes, 8):
        x = gram_ref[i % (modes // 2) : i % (modes // 2) + 8, :]
        x = x if i < modes // 2 else pltpu.roll(x, modes, 1)
        parts.append(jnp.where(lane < modes, x, jnp.where(lane == row + (i + modes), 1.0, 0.0)))
    pivots = []
    for k in range(0, modes, STEP):
        g, r = k // 8, k % 8
        steps = range(STEP)
        rows = [parts[g][r + i : r + i + 1, :] for i in steps]
        block = [[jnp.broadcast_to(x[:, k + i : k + i + 1], x.shape) for i in steps] for x in rows]
        inverses = []
        for i in steps:
            inverses.append(1.0 / block[i][i])
            for j in range(i + 1, STEP):
                ratio = block[j][i] * inverses[i]
                block[j] = [x - ratio * y for x, y in zip(block[j], block[i])]
                rows[j] = rows[j] - ratio * rows[i]
            pivots.append(block[i][i])
        scaled = [x * inverse for x, inverse in zip(rows, inverses)]
        for n in range(g, modes // 8):
            part = parts[n]
            columns = [jnp.broadcast_to(part[:, k + i : k + i + 1], part.shape) for i in steps]
            for i in steps:
                for j in range(i + 1, STEP):
                    columns[j] = columns[j] - columns[i] * (block[i][j] * inverses[i])
            for i in steps:
                column = jnp.where(row >= r + STEP, columns[i], 0.0) if n == g else columns[i]
                part = part - column * scaled[i]
            if n == g:
                for i in steps:
                    part = jnp.where(row == r + i, rows[i], part)
            parts[n] = part
    for i in range(modes // 8):
        scale = 1.0 / jnp.sqrt(jnp.concatenate(pivots[i * 8 : (i + 1) * 8], axis=0))
        part = parts[i] * scale
        upper = jnp.where(lane >= row + i * 8, part / norm, 0.0)
        factor_ref[i * 8 : (i + 1) * 8, :] = upper[:, :modes]
        part = part * norm
        inverse_ref[i * 8 : (i + 1) * 8, :] = jnp.where(lane < modes, pltpu.roll(part, modes, 1), part)
    lhs = jnp.concatenate(split2(inverse_ref[...]), axis=0)
    copies = []
    for v in range(VARS):
        both = dot(lhs, field_ref[2 * v * modes : (2 * v + 2) * modes, :])
        held_ref[v] = both[:modes] + both[modes:]
        copies.append(pltpu.make_async_copy(held_ref.at[v], out_ref.at[v], done_ref.at[v]))
        copies[-1].start()
    for copy in copies:
        copy.wait()


def local(mode_shapes, wall_coupling, owner_dev, owner_cell, neighbours, coupling_blocks, inv_blocks):
    devices = lax.axis_size("slab")
    cells = inv_blocks.shape[2]
    nodes, modes = mode_shapes.shape[0], mode_shapes.shape[1] // 3
    cap = max(2, 2 * nodes // devices)
    rim = cells // 8
    groups = 128 // cap
    columns = 3 * modes + 3 * VARS + 1
    rows = round_up(-(-columns // groups), 8)
    rows16 = round_up(rows, 16)
    packed = call(
        functools.partial(pack_body, cap, groups, rows),
        jax.ShapeDtypeStruct((devices * rows, 128), F32),
        mode_shapes.T, wall_coupling.T, owner_dev.T, owner_cell[None, :],
        grid=(1,),
        in_specs=[pl.BlockSpec((n, nodes), lambda i: (0, 0)) for n in (3 * modes, 3 * VARS, 1, 1)],
        out_specs=pl.BlockSpec((devices * rows, 128), lambda i: (0, 0)),
        scratch=[pltpu.VMEM(((groups - 1) * rows + rows16, nodes), F32), pltpu.VMEM((groups, 2 * rows16, nodes), BF16)],
        name="pack", limit=60,
    )
    arrived = lax.all_to_all(packed, "slab", split_axis=0, concat_axis=0, tiled=True)
    field = jax.ShapeDtypeStruct((VARS, modes, cells), F32)
    field_two = jax.ShapeDtypeStruct((VARS * 2 * modes, cells), BF16)
    edge = jax.ShapeDtypeStruct((VARS, modes, rim), F32)
    blocks, place = call(
        functools.partial(prepare_body, rim),
        (jax.ShapeDtypeStruct((VARS * VARS * 8, cells), F32), jax.ShapeDtypeStruct((8, cells), I32)),
        (lax.axis_index("slab") * cells).astype(I32)[None], neighbours, coupling_blocks.transpose(1, 2, 0, 3), inv_blocks,
        in_specs=[pl.BlockSpec(memory_space=pltpu.SMEM)] + [VMEM] * 3,
        cost_estimate=pl.CostEstimate(flops=10**9, bytes_accessed=10**7, transcendentals=0),
        name="prepare",
    )
    start, two, first, final = call(
        functools.partial(forcing_body, cap, groups, rows, modes, rim),
        (field, field_two, edge, edge),
        arrived, inv_blocks,
        scratch=[
            pltpu.VMEM((groups * rows, devices * cap), F32),
            pltpu.VMEM((VARS * 2 * modes, devices * cap), BF16),
            pltpu.VMEM((devices * cap, 128), F32),
        ],
        name="forcing",
    )
    up = [(i, i + 1) for i in range(devices - 1)]
    down = [(j, i) for i, j in up]
    x = start
    inner = cells - 2 * rim
    mid = jax.ShapeDtypeStruct((VARS, modes, inner), F32)
    mid_two = jax.ShapeDtypeStruct((VARS * 2 * modes, inner), BF16)
    fetched = [
        pltpu.VMEM((VARS * 2 * modes, (NBR - BY_LANES) * 256), F32), pltpu.VMEM((2, VARS, modes, 128), F32)
    ]
    cost = pl.CostEstimate(flops=10**10, bytes_accessed=3 * 10**7, transcendentals=0)
    for last in (False, True):
        before = lax.ppermute(final, "slab", up)
        after = lax.ppermute(first, "slab", down)
        middle = call(
            functools.partial(inner_body, rim, last), (mid_two,) if last else (mid, mid_two),
            x, two, start, place, blocks, scratch=fetched, cost_estimate=cost, name="inner_last" if last else "inner",
        )
        windows = [
            pltpu.VMEM((2, VARS, modes, 256 + 2 * rim), F32), pltpu.VMEM((2, VARS * 2 * modes, 256 + 2 * rim), BF16)
        ]
        if last:
            two, gram = call(
                functools.partial(outer_body, rim, last), (field_two, jax.ShapeDtypeStruct((modes // 2, 2 * modes), F32)),
                x, two, before, after, start, place, blocks, *middle,
                scratch=windows + fetched, name="outer_last",
            )
        else:
            x, two, first, final = call(
                functools.partial(outer_body, rim, last), (field, field_two, edge, edge),
                x, two, before, after, start, place, blocks, *middle, scratch=windows + fetched, name="outer",
            )
    reach = 1
    while reach < devices:
        gram = gram + lax.ppermute(gram, "slab", [(i, i ^ reach) for i in range(devices)])
        reach *= 2
    norm = math.sqrt(VARS * cells * devices)
    return call(
        functools.partial(basis_body, norm),
        (jax.ShapeDtypeStruct((VARS, modes, cells), F32), jax.ShapeDtypeStruct((modes, modes), F32)),
        gram, two,
        out_specs=(pl.BlockSpec(memory_space=pl.ANY), VMEM),
        scratch=[
            pltpu.VMEM((modes, 2 * modes), F32), pltpu.VMEM((VARS, modes, cells), F32), pltpu.SemaphoreType.DMA((VARS,))
        ],
        name="basis",
    )


def solution(mesh):
    in_specs = (
        P(("groups", "slab"), None),
        P(("groups", "slab"), None),
        P(("groups", "slab"), None),
        P(("groups", "slab")),
        P(None, ("groups", "slab")),
        P(None, None, None, ("groups", "slab")),
        P(None, None, ("groups", "slab")),
    )
    out_specs = (P(None, None, ("groups", "slab")), P("groups", None))
    return jax.shard_map(local, mesh=mesh, in_specs=in_specs, out_specs=out_specs, check_vma=False)
```

```python
import functools
import math

import jax
import jax.numpy as jnp
from jax import lax
from jax.experimental import pallas as pl
from jax.experimental.pallas import tpu as pltpu
from jax.sharding import PartitionSpec as P

VARS = 5
NBR = 6
BY_LANES = 2
ROWS = 32
ORDER = (("F", 0), ("L", 0), ("F", 1), ("L", 1), ("D", 0), ("D", 1))
LIMIT = 16
MANY = 8
STEP = 8
F32, BF16, I32 = jnp.float32, jnp.bfloat16, jnp.int32
VMEM = pl.BlockSpec(memory_space=pltpu.VMEM)


def round_up(value, unit):
    return -(-value // unit) * unit


def split2(x):
    high = x.astype(BF16)
    return high, (x - high.astype(F32)).astype(BF16)


def dot(a, b):
    return jnp.dot(a, b, preferred_element_type=F32)


def call(body, out_shape, *args, name, scratch=(), limit=LIMIT, flops=0, **kw):
    return pl.pallas_call(
        body,
        out_shape=out_shape,
        in_specs=kw.pop("in_specs", [VMEM] * len(args)),
        out_specs=kw.pop("out_specs", jax.tree.map(lambda _: VMEM, out_shape)),
        scratch_shapes=list(scratch),
        name=name,
        compiler_params=pltpu.CompilerParams(vmem_limit_bytes=limit << 20),
        **kw,
    )(*args)


def pack_body(cap, groups, rows, shapes_ref, weights_ref, dev_ref, cell_ref, out_ref, rows_ref, lhs_ref):
    width, nodes = shapes_ref.shape
    devices = out_ref.shape[0] // rows
    rows16 = lhs_ref.shape[1] // 2
    used = width + weights_ref.shape[0]
    rows_ref[used - used % 8 :, :] = jnp.zeros((rows_ref.shape[0] - used + used % 8, nodes), F32)
    rows_ref[:width, :] = shapes_ref[...]
    rows_ref[width:used, :] = weights_ref[...]
    rows_ref[used : used + 1, :] = (cell_ref[...] + 1).astype(F32)
    for g in range(groups):
        x = rows_ref[g * rows : g * rows + rows16, :]
        lhs_ref[g, :rows16, :], lhs_ref[g, rows16:, :] = split2(x)
    dest = dev_ref[...]
    named = jnp.where(dest == lax.broadcasted_iota(I32, (devices, nodes), 0), 1.0, 0.0)
    earlier = jnp.where(
        lax.broadcasted_iota(I32, (nodes, nodes), 0) < lax.broadcasted_iota(I32, (nodes, nodes), 1), 1.0, 0.0
    )
    rank = jnp.sum(named * dot(named.astype(BF16), earlier.astype(BF16)), axis=0, keepdims=True).astype(I32)
    place = dest * 128 + rank
    column = jnp.broadcast_to(place.astype(F32), (8, nodes)).T[:, :1]
    place = jnp.broadcast_to(column, (nodes, 128)).astype(I32)
    lane = lax.broadcasted_iota(I32, (nodes, 128), 1)

    def several(step, _):
        total = jnp.zeros((2 * rows16, 128 * MANY), F32)
        for g in range(groups):
            hot = [
                jnp.where(place + (g * cap - (step * MANY + h) * 128) == lane, 1.0, 0.0).astype(BF16)
                for h in range(MANY)
            ]
            total = total + dot(lhs_ref[g], jnp.concatenate(hot, axis=1))
        total = total[:rows16] + total[rows16:]
        for h in range(MANY):
            at = pl.multiple_of((step * MANY + h) * rows, 8)
            out_ref[pl.ds(at, rows), :] = total[:rows, h * 128 : (h + 1) * 128]
        return 0

    lax.fori_loop(0, devices // MANY, several, 0)


def prepare_body(rim, first_ref, neighbours_ref, coupling_ref, inv_ref, blocks_ref, place_ref):
    cells = neighbours_ref.shape[1]
    near = neighbours_ref[...]
    filled = near >= 0
    for u in range(VARS):
        for v in range(VARS):
            total = inv_ref[v, 0:1, :] * coupling_ref[0, u]
            for w in range(1, VARS):
                total = total + inv_ref[v, w : w + 1, :] * coupling_ref[w, u]
            blocks_ref[(v * VARS + u) * 8 : (v * VARS + u) * 8 + NBR, :] = jnp.where(filled, total, 0.0)
    base = lax.broadcasted_iota(I32, (NBR, cells), 1) // 256 * 256 + first_ref[0]
    place_ref[:NBR, :] = jnp.where(filled, near + rim - base, rim)


def forcing_body(cap, groups, rows, modes, rim, arrived_ref, inv_ref, out_ref, two_ref, first_ref, last_ref, table_ref, lhs_ref, tag_ref):
    devices = arrived_ref.shape[0] // rows
    slots = devices * cap
    cells = out_ref.shape[2]
    lane_group = lax.broadcasted_iota(I32, (rows, 128), 1) // cap
    for p in range(devices // groups):
        chunks = [arrived_ref[(p * groups + b) * rows : (p * groups + b + 1) * rows, :] for b in range(groups)]
        for g in range(groups):
            merged = chunks[g]
            for b in range(groups):
                if b != g:
                    turned = pltpu.roll(chunks[b], (b - g) * cap % 128, 1)
                    merged = jnp.where(lane_group == b, turned, merged)
            table_ref[g * rows : (g + 1) * rows, p * 128 : (p + 1) * 128] = merged
    at = 3 * modes
    tag_row = at + 3 * VARS
    tags = table_ref[tag_row // 8 * 8 : tag_row // 8 * 8 + 8, :].T
    tag_ref[...] = jnp.broadcast_to(tags[:, tag_row % 8 : tag_row % 8 + 1], (slots, 128))
    for v in range(VARS):
        load = table_ref[at + 3 * v : at + 3 * v + 1, :] * table_ref[:modes, :]
        for k in range(1, 3):
            load = load + table_ref[at + 3 * v + k : at + 3 * v + k + 1, :] * table_ref[k * modes : (k + 1) * modes, :]
        high, low = split2(load)
        lhs_ref[v * 2 * modes : v * 2 * modes + modes, :] = high
        lhs_ref[v * 2 * modes + modes : (v + 1) * 2 * modes, :] = low
    lane = lax.broadcasted_iota(I32, (slots, 128), 1) + 1

    def tile(t, _):
        lo = pl.multiple_of(t * 1024, 1024)
        hot = [jnp.where(tag_ref[...] == (lane + (lo + h * 128)).astype(F32), 1.0, 0.0).astype(BF16) for h in range(8)]
        both = dot(lhs_ref[...], jnp.concatenate(hot, axis=1))
        forcing = [both[u * 2 * modes : u * 2 * modes + modes] + both[u * 2 * modes + modes : (u + 1) * 2 * modes] for u in range(VARS)]
        for v in range(VARS):
            total = inv_ref[v, 0:1, pl.ds(lo, 1024)] * forcing[0]
            for u in range(1, VARS):
                total = total + inv_ref[v, u : u + 1, pl.ds(lo, 1024)] * forcing[u]
            out_ref[v, :, pl.ds(lo, 1024)] = total
            high, low = split2(total)
            two_ref[2 * v * modes : (2 * v + 1) * modes, pl.ds(lo, 1024)] = high
            two_ref[(2 * v + 1) * modes : (2 * v + 2) * modes, pl.ds(lo, 1024)] = low
        return 0

    lax.fori_loop(0, cells // 1024, tile, 0)
    first_ref[...] = out_ref[:, :, :rim]
    last_ref[...] = out_ref[:, :, cells - rim :]


def relax(fetched_ref, part_ref, two, source, start_ref, place_ref, blocks_ref, lo, store):
    modes = start_ref.shape[1]
    by_matmul = NBR - BY_LANES
    rows = range(0, ROWS, 8)
    two_ref, first = two

    def subtract(acc, at, j, u, values):
        for v in range(VARS):
            row = (v * VARS + u) * 8 + j
            block = blocks_ref[row : row + 1, pl.ds(at, 128)]
            acc[v] = [a - block * value for a, value in zip(acc[v], values)]

    def fetch(h):
        at = pl.multiple_of(lo + h * 128, 128)
        row = lax.broadcasted_iota(I32, (640, 128), 0) + h * 128
        hot = [jnp.where(row == place_ref[j : j + 1, pl.ds(at, 128)], 1.0, 0.0).astype(BF16) for j in range(by_matmul)]
        window = pl.ds(pl.multiple_of(first + h * 128, 128), 640)
        fetched_ref[:, h * by_matmul * 128 : (h + 1) * by_matmul * 128] = dot(two_ref[:, window], jnp.concatenate(hot, axis=1))

    def lanes(h):
        at = pl.multiple_of(lo + h * 128, 128)
        picks = []
        for j in range(by_matmul, NBR):
            place = jnp.broadcast_to(place_ref[j : j + 1, pl.ds(at, 128)] - h * 128, (8, 128))
            picks.append((j, place & 127, place >> 7))
        for m in range(0, modes, ROWS):
            acc = [[start_ref[v, m + i : m + i + 8, pl.ds(at, 128)] for i in rows] for v in range(VARS)]
            for u in range(VARS):
                around = [[source(u, m + i, h + s) for s in range(5)] for i in rows]
                taken = [
                    [[jnp.take_along_axis(x, lane, axis=1, mode="promise_in_bounds") for x in blocks] for blocks in around]
                    for _, lane, _ in picks
                ]
                for (j, _, where), found in zip(picks, taken):
                    values = []
                    for x in found:
                        value = x[0]
                        for s in range(1, 5):
                            value = jnp.where(where == s, x[s], value)
                        values.append(value)
                    subtract(acc, at, j, u, values)
            for v in range(VARS):
                for n, i in enumerate(rows):
                    part_ref[h, v, m + i : m + i + 8, :] = acc[v][n]

    def dots(h):
        at = pl.multiple_of(lo + h * 128, 128)
        for m in range(0, modes, ROWS):
            acc = [[part_ref[h, v, m + i : m + i + 8, :] for i in rows] for v in range(VARS)]
            for u in range(VARS):
                for j in range(by_matmul):
                    values = []
                    for i in rows:
                        r, c = u * 2 * modes + m + i, (h * by_matmul + j) * 128
                        values.append(
                            fetched_ref[r : r + 8, c : c + 128] + fetched_ref[r + modes : r + modes + 8, c : c + 128]
                        )
                    subtract(acc, at, j, u, values)
            for v in range(VARS):
                store(v, m, h, jnp.concatenate(acc[v], axis=0))

    for step, h in ORDER:
        {"F": fetch, "L": lanes, "D": dots}[step](h)


def put_two(two_ref, modes, v, m, at, high, low):
    value_rows = high.shape[0]
    two_ref[2 * v * modes + m : 2 * v * modes + m + value_rows, at] = high
    two_ref[(2 * v + 1) * modes + m : (2 * v + 1) * modes + m + value_rows, at] = low


def inner_body(rim, last, x_ref, two_ref, start_ref, place_ref, blocks_ref, *refs):
    if last:
        mid_two_ref, fetched_ref, part_ref = refs
    else:
        mid_ref, mid_two_ref, fetched_ref, part_ref = refs
    modes, cells = x_ref.shape[1:]
    tiles = (cells - 2 * rim) // 256

    def one_tile(t, _):
        lo = pl.multiple_of(rim + t * 256, 256)

        def store(v, m, h, value):
            at = pl.ds(pl.multiple_of(t * 256 + h * 128, 128), 128)
            if not last:
                mid_ref[v, m : m + ROWS, at] = value
            put_two(mid_two_ref, modes, v, m, at, *split2(value))

        def source(u, m, s):
            return x_ref[u, m : m + 8, pl.ds(pl.multiple_of(lo - rim + s * 128, 128), 128)]

        two = (two_ref, pl.multiple_of(lo - rim, 256))
        relax(fetched_ref, part_ref, two, source, start_ref, place_ref, blocks_ref, lo, store)
        return 0

    lax.fori_loop(0, tiles, one_tile, 0)


def outer_body(rim, last, x_ref, two_ref, before_ref, after_ref, start_ref, place_ref, blocks_ref, *refs):
    if last:
        mid_two_ref, out_two_ref, gram_ref, window_ref, window_two_ref, fetched_ref, part_ref = refs
    else:
        mid_ref, mid_two_ref, out_ref, out_two_ref, first_ref, last_ref, window_ref, window_two_ref, fetched_ref, part_ref = refs
    modes, cells = x_ref.shape[1:]
    ends = cells - rim
    near = 256 + rim
    window_ref[0, :, :, :rim] = before_ref[...]
    window_ref[0, :, :, rim:] = x_ref[:, :, :near]
    window_ref[1, :, :, :near] = x_ref[:, :, cells - near :]
    window_ref[1, :, :, near:] = after_ref[...]
    window_two_ref[0, :, rim:] = two_ref[:, :near]
    window_two_ref[1, :, :near] = two_ref[:, cells - near :]
    for side, (ref, at) in enumerate(((before_ref, 0), (after_ref, near))):
        for u in range(VARS):
            high, low = split2(ref[u])
            window_two_ref[side, 2 * u * modes : (2 * u + 1) * modes, at : at + rim] = high
            window_two_ref[side, (2 * u + 1) * modes : (2 * u + 2) * modes, at : at + rim] = low
    out_two_ref[:, rim:ends] = mid_two_ref[...]
    if not last:
        out_ref[:, :, rim:ends] = mid_ref[...]

    def one_side(t, _):
        lo = pl.multiple_of(t * ends, 256)

        def source(u, m, s):
            return window_ref[t, u, m : m + 8, s * 128 : (s + 1) * 128]

        def store(v, m, h, value):
            at = pl.ds(pl.multiple_of(lo + h * 128, 128), 128)
            if not last:
                out_ref[v, m : m + ROWS, at] = value
            put_two(out_two_ref, modes, v, m, at, *split2(value))

        two = (window_two_ref.at[t], 0)
        relax(fetched_ref, part_ref, two, source, start_ref, place_ref, blocks_ref, lo, store)
        return 0

    lax.fori_loop(0, 2, one_side, 0)
    if not last:
        first_ref[...] = out_ref[:, :, :rim]
        last_ref[...] = out_ref[:, :, ends:]
    if last:
        gram = jnp.zeros((2 * modes, 2 * modes), F32)
        for v in range(VARS):
            both = out_two_ref[2 * v * modes : (2 * v + 2) * modes, :]
            gram = gram + lax.dot_general(both, both, (((1,), (1,)), ((), ())), preferred_element_type=F32)
        gram = gram[:modes] + gram[modes:]
        gram = gram + pltpu.roll(gram, modes, 1)
        half = modes // 2
        gram_ref[...] = jnp.where(lax.broadcasted_iota(I32, (half, 2 * modes), 1) < modes, gram[:half], gram[half:])


def basis_body(norm, gram_ref, field_ref, out_ref, factor_ref, inverse_ref, held_ref, done_ref):
    modes = factor_ref.shape[0]
    row = lax.broadcasted_iota(I32, (8, 2 * modes), 0)
    lane = lax.broadcasted_iota(I32, (8, 2 * modes), 1)
    parts = []
    for i in range(0, modes, 8):
        x = gram_ref[i % (modes // 2) : i % (modes // 2) + 8, :]
        x = x if i < modes // 2 else pltpu.roll(x, modes, 1)
        parts.append(jnp.where(lane < modes, x, jnp.where(lane == row + (i + modes), 1.0, 0.0)))
    pivots = []
    for k in range(0, modes, STEP):
        g, r = k // 8, k % 8
        steps = range(STEP)
        rows = [parts[g][r + i : r + i + 1, :] for i in steps]
        block = [[jnp.broadcast_to(x[:, k + i : k + i + 1], x.shape) for i in steps] for x in rows]
        inverses = []
        for i in steps:
            inverses.append(1.0 / block[i][i])
            for j in range(i + 1, STEP):
                ratio = block[j][i] * inverses[i]
                block[j] = [x - ratio * y for x, y in zip(block[j], block[i])]
                rows[j] = rows[j] - ratio * rows[i]
            pivots.append(block[i][i])
        scaled = [x * inverse for x, inverse in zip(rows, inverses)]
        for n in range(g, modes // 8):
            part = parts[n]
            columns = [jnp.broadcast_to(part[:, k + i : k + i + 1], part.shape) for i in steps]
            for i in steps:
                for j in range(i + 1, STEP):
                    columns[j] = columns[j] - columns[i] * (block[i][j] * inverses[i])
            for i in steps:
                column = jnp.where(row >= r + STEP, columns[i], 0.0) if n == g else columns[i]
                part = part - column * scaled[i]
            if n == g:
                for i in steps:
                    part = jnp.where(row == r + i, rows[i], part)
            parts[n] = part
    for i in range(modes // 8):
        scale = 1.0 / jnp.sqrt(jnp.concatenate(pivots[i * 8 : (i + 1) * 8], axis=0))
        part = parts[i] * scale
        upper = jnp.where(lane >= row + i * 8, part / norm, 0.0)
        factor_ref[i * 8 : (i + 1) * 8, :] = upper[:, :modes]
        part = part * norm
        inverse_ref[i * 8 : (i + 1) * 8, :] = jnp.where(lane < modes, pltpu.roll(part, modes, 1), part)
    lhs = jnp.concatenate(split2(inverse_ref[...]), axis=0)
    copies = []
    for v in range(VARS):
        both = dot(lhs, field_ref[2 * v * modes : (2 * v + 2) * modes, :])
        held_ref[v] = both[:modes] + both[modes:]
        copies.append(pltpu.make_async_copy(held_ref.at[v], out_ref.at[v], done_ref.at[v]))
        copies[-1].start()
    for copy in copies:
        copy.wait()


def local(mode_shapes, wall_coupling, owner_dev, owner_cell, neighbours, coupling_blocks, inv_blocks):
    devices = lax.axis_size("slab")
    cells = inv_blocks.shape[2]
    nodes, modes = mode_shapes.shape[0], mode_shapes.shape[1] // 3
    cap = max(2, 2 * nodes // devices)
    rim = cells // 8
    groups = 128 // cap
    columns = 3 * modes + 3 * VARS + 1
    rows = round_up(-(-columns // groups), 8)
    rows16 = round_up(rows, 16)
    packed = call(
        functools.partial(pack_body, cap, groups, rows),
        jax.ShapeDtypeStruct((devices * rows, 128), F32),
        mode_shapes.T, wall_coupling.T, owner_dev.T, owner_cell[None, :],
        grid=(1,),
        in_specs=[pl.BlockSpec((n, nodes), lambda i: (0, 0)) for n in (3 * modes, 3 * VARS, 1, 1)],
        out_specs=pl.BlockSpec((devices * rows, 128), lambda i: (0, 0)),
        scratch=[pltpu.VMEM(((groups - 1) * rows + rows16, nodes), F32), pltpu.VMEM((groups, 2 * rows16, nodes), BF16)],
        name="pack", limit=60,
    )
    arrived = lax.all_to_all(packed, "slab", split_axis=0, concat_axis=0, tiled=True)
    field = jax.ShapeDtypeStruct((VARS, modes, cells), F32)
    field_two = jax.ShapeDtypeStruct((VARS * 2 * modes, cells), BF16)
    edge = jax.ShapeDtypeStruct((VARS, modes, rim), F32)
    blocks, place = call(
        functools.partial(prepare_body, rim),
        (jax.ShapeDtypeStruct((VARS * VARS * 8, cells), F32), jax.ShapeDtypeStruct((8, cells), I32)),
        (lax.axis_index("slab") * cells).astype(I32)[None], neighbours, coupling_blocks.transpose(1, 2, 0, 3), inv_blocks,
        in_specs=[pl.BlockSpec(memory_space=pltpu.SMEM)] + [VMEM] * 3,
        cost_estimate=pl.CostEstimate(flops=10**9, bytes_accessed=10**7, transcendentals=0),
        name="prepare",
    )
    start, two, first, final = call(
        functools.partial(forcing_body, cap, groups, rows, modes, rim),
        (field, field_two, edge, edge),
        arrived, inv_blocks,
        scratch=[
            pltpu.VMEM((groups * rows, devices * cap), F32),
            pltpu.VMEM((VARS * 2 * modes, devices * cap), BF16),
            pltpu.VMEM((devices * cap, 128), F32),
        ],
        name="forcing",
    )
    up = [(i, i + 1) for i in range(devices - 1)]
    down = [(j, i) for i, j in up]
    x = start
    inner = cells - 2 * rim
    mid = jax.ShapeDtypeStruct((VARS, modes, inner), F32)
    mid_two = jax.ShapeDtypeStruct((VARS * 2 * modes, inner), BF16)
    fetched = [
        pltpu.VMEM((VARS * 2 * modes, (NBR - BY_LANES) * 256), F32), pltpu.VMEM((2, VARS, modes, 128), F32)
    ]
    cost = pl.CostEstimate(flops=10**10, bytes_accessed=3 * 10**7, transcendentals=0)
    for last in (False, True):
        before = lax.ppermute(final, "slab", up)
        after = lax.ppermute(first, "slab", down)
        middle = call(
            functools.partial(inner_body, rim, last), (mid_two,) if last else (mid, mid_two),
            x, two, start, place, blocks, scratch=fetched, cost_estimate=cost, name="inner_last" if last else "inner",
        )
        windows = [
            pltpu.VMEM((2, VARS, modes, 256 + 2 * rim), F32), pltpu.VMEM((2, VARS * 2 * modes, 256 + 2 * rim), BF16)
        ]
        if last:
            two, gram = call(
                functools.partial(outer_body, rim, last), (field_two, jax.ShapeDtypeStruct((modes // 2, 2 * modes), F32)),
                x, two, before, after, start, place, blocks, *middle,
                scratch=windows + fetched, name="outer_last",
            )
        else:
            x, two, first, final = call(
                functools.partial(outer_body, rim, last), (field, field_two, edge, edge),
                x, two, before, after, start, place, blocks, *middle, scratch=windows + fetched, name="outer",
            )
    reach = 1
    while reach < devices:
        gram = gram + lax.ppermute(gram, "slab", [(i, i ^ reach) for i in range(devices)])
        reach *= 2
    norm = math.sqrt(VARS * cells * devices)
    return call(
        functools.partial(basis_body, norm),
        (jax.ShapeDtypeStruct((VARS, modes, cells), F32), jax.ShapeDtypeStruct((modes, modes), F32)),
        gram, two,
        out_specs=(pl.BlockSpec(memory_space=pl.ANY), VMEM),
        scratch=[
            pltpu.VMEM((modes, 2 * modes), F32), pltpu.VMEM((VARS, modes, cells), F32), pltpu.SemaphoreType.DMA((VARS,))
        ],
        name="basis",
    )


def solution(mesh):
    in_specs = (
        P(("groups", "slab"), None),
        P(("groups", "slab"), None),
        P(("groups", "slab"), None),
        P(("groups", "slab")),
        P(None, ("groups", "slab")),
        P(None, None, None, ("groups", "slab")),
        P(None, None, ("groups", "slab")),
    )
    out_specs = (P(None, None, ("groups", "slab")), P("groups", None))
    return jax.shard_map(local, mesh=mesh, in_specs=in_specs, out_specs=out_specs, check_vma=False)
```

```python
import functools
import math

import jax
import jax.numpy as jnp
from jax import lax
from jax.experimental import pallas as pl
from jax.experimental.pallas import tpu as pltpu
from jax.sharding import PartitionSpec as P

VARS = 5
NBR = 6
BY_LANES = 2
ROWS = 32
ORDER = (("F", 0), ("L", 0), ("F", 1), ("L", 1), ("D", 0), ("D", 1))
LIMIT = 16
MANY = 8
STEP = 8
F32, BF16, I32 = jnp.float32, jnp.bfloat16, jnp.int32
VMEM = pl.BlockSpec(memory_space=pltpu.VMEM)


def round_up(value, unit):
    return -(-value // unit) * unit


def split2(x):
    high = x.astype(BF16)
    return high, (x - high.astype(F32)).astype(BF16)


def dot(a, b):
    return jnp.dot(a, b, preferred_element_type=F32)


def call(body, out_shape, *args, name, scratch=(), limit=LIMIT, flops=0, **kw):
    return pl.pallas_call(
        body,
        out_shape=out_shape,
        in_specs=kw.pop("in_specs", [VMEM] * len(args)),
        out_specs=kw.pop("out_specs", jax.tree.map(lambda _: VMEM, out_shape)),
        scratch_shapes=list(scratch),
        name=name,
        compiler_params=pltpu.CompilerParams(vmem_limit_bytes=limit << 20),
        **kw,
    )(*args)


def pack_body(cap, groups, rows, shapes_ref, weights_ref, dev_ref, cell_ref, out_ref, rows_ref, lhs_ref):
    width, nodes = shapes_ref.shape
    devices = out_ref.shape[0] // rows
    rows16 = lhs_ref.shape[1] // 2
    used = width + weights_ref.shape[0]
    rows_ref[used - used % 8 :, :] = jnp.zeros((rows_ref.shape[0] - used + used % 8, nodes), F32)
    rows_ref[:width, :] = shapes_ref[...]
    rows_ref[width:used, :] = weights_ref[...]
    rows_ref[used : used + 1, :] = (cell_ref[...] + 1).astype(F32)
    for g in range(groups):
        x = rows_ref[g * rows : g * rows + rows16, :]
        lhs_ref[g, :rows16, :], lhs_ref[g, rows16:, :] = split2(x)
    dest = dev_ref[...]
    named = jnp.where(dest == lax.broadcasted_iota(I32, (devices, nodes), 0), 1.0, 0.0)
    earlier = jnp.where(
        lax.broadcasted_iota(I32, (nodes, nodes), 0) < lax.broadcasted_iota(I32, (nodes, nodes), 1), 1.0, 0.0
    )
    rank = jnp.sum(named * dot(named.astype(BF16), earlier.astype(BF16)), axis=0, keepdims=True).astype(I32)
    place = dest * 128 + rank
    column = jnp.broadcast_to(place.astype(F32), (8, nodes)).T[:, :1]
    place = jnp.broadcast_to(column, (nodes, 128)).astype(I32)
    lane = lax.broadcasted_iota(I32, (nodes, 128), 1)

    def several(step, _):
        total = jnp.zeros((2 * rows16, 128 * MANY), F32)
        for g in range(groups):
            hot = [
                jnp.where(place + (g * cap - (step * MANY + h) * 128) == lane, 1.0, 0.0).astype(BF16)
                for h in range(MANY)
            ]
            total = total + dot(lhs_ref[g], jnp.concatenate(hot, axis=1))
        total = total[:rows16] + total[rows16:]
        for h in range(MANY):
            at = pl.multiple_of((step * MANY + h) * rows, 8)
            out_ref[pl.ds(at, rows), :] = total[:rows, h * 128 : (h + 1) * 128]
        return 0

    lax.fori_loop(0, devices // MANY, several, 0)


def prepare_body(rim, first_ref, neighbours_ref, coupling_ref, inv_ref, blocks_ref, place_ref):
    cells = neighbours_ref.shape[1]
    near = neighbours_ref[...]
    filled = near >= 0
    for u in range(VARS):
        for v in range(VARS):
            total = inv_ref[v, 0:1, :] * coupling_ref[0, u]
            for w in range(1, VARS):
                total = total + inv_ref[v, w : w + 1, :] * coupling_ref[w, u]
            blocks_ref[(v * VARS + u) * 8 : (v * VARS + u) * 8 + NBR, :] = jnp.where(filled, total, 0.0)
    base = lax.broadcasted_iota(I32, (NBR, cells), 1) // 256 * 256 + first_ref[0]
    place_ref[:NBR, :] = jnp.where(filled, near + rim - base, rim)


def forcing_body(cap, groups, rows, modes, rim, arrived_ref, inv_ref, out_ref, two_ref, first_ref, last_ref, table_ref, lhs_ref, tag_ref):
    devices = arrived_ref.shape[0] // rows
    slots = devices * cap
    cells = out_ref.shape[2]
    lane_group = lax.broadcasted_iota(I32, (rows, 128), 1) // cap
    for p in range(devices // groups):
        chunks = [arrived_ref[(p * groups + b) * rows : (p * groups + b + 1) * rows, :] for b in range(groups)]
        for g in range(groups):
            merged = chunks[g]
            for b in range(groups):
                if b != g:
                    turned = pltpu.roll(chunks[b], (b - g) * cap % 128, 1)
                    merged = jnp.where(lane_group == b, turned, merged)
            table_ref[g * rows : (g + 1) * rows, p * 128 : (p + 1) * 128] = merged
    at = 3 * modes
    tag_row = at + 3 * VARS
    tags = table_ref[tag_row // 8 * 8 : tag_row // 8 * 8 + 8, :].T
    tag_ref[...] = jnp.broadcast_to(tags[:, tag_row % 8 : tag_row % 8 + 1], (slots, 128))
    for v in range(VARS):
        load = table_ref[at + 3 * v : at + 3 * v + 1, :] * table_ref[:modes, :]
        for k in range(1, 3):
            load = load + table_ref[at + 3 * v + k : at + 3 * v + k + 1, :] * table_ref[k * modes : (k + 1) * modes, :]
        high, low = split2(load)
        lhs_ref[v * 2 * modes : v * 2 * modes + modes, :] = high
        lhs_ref[v * 2 * modes + modes : (v + 1) * 2 * modes, :] = low
    lane = lax.broadcasted_iota(I32, (slots, 128), 1) + 1

    def tile(t, _):
        lo = pl.multiple_of(t * 1024, 1024)
        hot = [jnp.where(tag_ref[...] == (lane + (lo + h * 128)).astype(F32), 1.0, 0.0).astype(BF16) for h in range(8)]
        both = dot(lhs_ref[...], jnp.concatenate(hot, axis=1))
        forcing = [both[u * 2 * modes : u * 2 * modes + modes] + both[u * 2 * modes + modes : (u + 1) * 2 * modes] for u in range(VARS)]
        for v in range(VARS):
            total = inv_ref[v, 0:1, pl.ds(lo, 1024)] * forcing[0]
            for u in range(1, VARS):
                total = total + inv_ref[v, u : u + 1, pl.ds(lo, 1024)] * forcing[u]
            out_ref[v, :, pl.ds(lo, 1024)] = total
            high, low = split2(total)
            two_ref[2 * v * modes : (2 * v + 1) * modes, pl.ds(lo, 1024)] = high
            two_ref[(2 * v + 1) * modes : (2 * v + 2) * modes, pl.ds(lo, 1024)] = low
        return 0

    lax.fori_loop(0, cells // 1024, tile, 0)
    first_ref[...] = out_ref[:, :, :rim]
    last_ref[...] = out_ref[:, :, cells - rim :]


def relax(fetched_ref, part_ref, two, source, start_ref, place_ref, blocks_ref, lo, store):
    modes = start_ref.shape[1]
    by_matmul = NBR - BY_LANES
    rows = range(0, ROWS, 8)
    two_ref, first = two

    def subtract(acc, at, j, u, values):
        for v in range(VARS):
            row = (v * VARS + u) * 8 + j
            block = blocks_ref[row : row + 1, pl.ds(at, 128)]
            acc[v] = [a - block * value for a, value in zip(acc[v], values)]

    def fetch(h):
        at = pl.multiple_of(lo + h * 128, 128)
        row = lax.broadcasted_iota(I32, (640, 128), 0) + h * 128
        hot = [jnp.where(row == place_ref[j : j + 1, pl.ds(at, 128)], 1.0, 0.0).astype(BF16) for j in range(by_matmul)]
        window = pl.ds(pl.multiple_of(first + h * 128, 128), 640)
        fetched_ref[:, h * by_matmul * 128 : (h + 1) * by_matmul * 128] = dot(two_ref[:, window], jnp.concatenate(hot, axis=1))

    def lanes(h):
        at = pl.multiple_of(lo + h * 128, 128)
        picks = []
        for j in range(by_matmul, NBR):
            place = jnp.broadcast_to(place_ref[j : j + 1, pl.ds(at, 128)] - h * 128, (8, 128))
            picks.append((j, place & 127, place >> 7))
        for m in range(0, modes, ROWS):
            acc = [[start_ref[v, m + i : m + i + 8, pl.ds(at, 128)] for i in rows] for v in range(VARS)]
            for u in range(VARS):
                around = [[source(u, m + i, h + s) for s in range(5)] for i in rows]
                taken = [
                    [[jnp.take_along_axis(x, lane, axis=1, mode="promise_in_bounds") for x in blocks] for blocks in around]
                    for _, lane, _ in picks
                ]
                for (j, _, where), found in zip(picks, taken):
                    values = []
                    for x in found:
                        value = x[0]
                        for s in range(1, 5):
                            value = jnp.where(where == s, x[s], value)
                        values.append(value)
                    subtract(acc, at, j, u, values)
            for v in range(VARS):
                for n, i in enumerate(rows):
                    part_ref[h, v, m + i : m + i + 8, :] = acc[v][n]

    def dots(h):
        at = pl.multiple_of(lo + h * 128, 128)
        for m in range(0, modes, ROWS):
            acc = [[part_ref[h, v, m + i : m + i + 8, :] for i in rows] for v in range(VARS)]
            for u in range(VARS):
                for j in range(by_matmul):
                    values = []
                    for i in rows:
                        r, c = u * 2 * modes + m + i, (h * by_matmul + j) * 128
                        values.append(
                            fetched_ref[r : r + 8, c : c + 128] + fetched_ref[r + modes : r + modes + 8, c : c + 128]
                        )
                    subtract(acc, at, j, u, values)
            for v in range(VARS):
                store(v, m, h, jnp.concatenate(acc[v], axis=0))

    for step, h in ORDER:
        {"F": fetch, "L": lanes, "D": dots}[step](h)


def put_two(two_ref, modes, v, m, at, high, low):
    value_rows = high.shape[0]
    two_ref[2 * v * modes + m : 2 * v * modes + m + value_rows, at] = high
    two_ref[(2 * v + 1) * modes + m : (2 * v + 1) * modes + m + value_rows, at] = low


def inner_body(rim, last, x_ref, two_ref, start_ref, place_ref, blocks_ref, *refs):
    if last:
        mid_two_ref, fetched_ref, part_ref = refs
    else:
        mid_ref, mid_two_ref, fetched_ref, part_ref = refs
    modes, cells = x_ref.shape[1:]
    tiles = (cells - 2 * rim) // 256

    def one_tile(t, _):
        lo = pl.multiple_of(rim + t * 256, 256)

        def store(v, m, h, value):
            at = pl.ds(pl.multiple_of(t * 256 + h * 128, 128), 128)
            if not last:
                mid_ref[v, m : m + ROWS, at] = value
            put_two(mid_two_ref, modes, v, m, at, *split2(value))

        def source(u, m, s):
            return x_ref[u, m : m + 8, pl.ds(pl.multiple_of(lo - rim + s * 128, 128), 128)]

        two = (two_ref, pl.multiple_of(lo - rim, 256))
        relax(fetched_ref, part_ref, two, source, start_ref, place_ref, blocks_ref, lo, store)
        return 0

    lax.fori_loop(0, tiles, one_tile, 0)


def outer_body(rim, last, x_ref, two_ref, before_ref, after_ref, start_ref, place_ref, blocks_ref, *refs):
    if last:
        mid_two_ref, out_two_ref, gram_ref, window_ref, window_two_ref, fetched_ref, part_ref = refs
    else:
        mid_ref, mid_two_ref, out_ref, out_two_ref, first_ref, last_ref, window_ref, window_two_ref, fetched_ref, part_ref = refs
    modes, cells = x_ref.shape[1:]
    ends = cells - rim
    near = 256 + rim
    window_ref[0, :, :, :rim] = before_ref[...]
    window_ref[0, :, :, rim:] = x_ref[:, :, :near]
    window_ref[1, :, :, :near] = x_ref[:, :, cells - near :]
    window_ref[1, :, :, near:] = after_ref[...]
    window_two_ref[0, :, rim:] = two_ref[:, :near]
    window_two_ref[1, :, :near] = two_ref[:, cells - near :]
    for side, (ref, at) in enumerate(((before_ref, 0), (after_ref, near))):
        for u in range(VARS):
            high, low = split2(ref[u])
            window_two_ref[side, 2 * u * modes : (2 * u + 1) * modes, at : at + rim] = high
            window_two_ref[side, (2 * u + 1) * modes : (2 * u + 2) * modes, at : at + rim] = low
    out_two_ref[:, rim:ends] = mid_two_ref[...]
    if not last:
        out_ref[:, :, rim:ends] = mid_ref[...]

    def one_side(t, _):
        lo = pl.multiple_of(t * ends, 256)

        def source(u, m, s):
            return window_ref[t, u, m : m + 8, s * 128 : (s + 1) * 128]

        def store(v, m, h, value):
            at = pl.ds(pl.multiple_of(lo + h * 128, 128), 128)
            if not last:
                out_ref[v, m : m + ROWS, at] = value
            put_two(out_two_ref, modes, v, m, at, *split2(value))

        two = (window_two_ref.at[t], 0)
        relax(fetched_ref, part_ref, two, source, start_ref, place_ref, blocks_ref, lo, store)
        return 0

    lax.fori_loop(0, 2, one_side, 0)
    if not last:
        first_ref[...] = out_ref[:, :, :rim]
        last_ref[...] = out_ref[:, :, ends:]
    if last:
        gram = jnp.zeros((2 * modes, 2 * modes), F32)
        for v in range(VARS):
            both = out_two_ref[2 * v * modes : (2 * v + 2) * modes, :]
            gram = gram + lax.dot_general(both, both, (((1,), (1,)), ((), ())), preferred_element_type=F32)
        gram = gram[:modes] + gram[modes:]
        gram = gram + pltpu.roll(gram, modes, 1)
        half = modes // 2
        gram_ref[...] = jnp.where(lax.broadcasted_iota(I32, (half, 2 * modes), 1) < modes, gram[:half], gram[half:])


def basis_body(norm, gram_ref, field_ref, out_ref, factor_ref, inverse_ref, held_ref, done_ref):
    modes = factor_ref.shape[0]
    row = lax.broadcasted_iota(I32, (8, 2 * modes), 0)
    lane = lax.broadcasted_iota(I32, (8, 2 * modes), 1)
    parts = []
    for i in range(0, modes, 8):
        x = gram_ref[i % (modes // 2) : i % (modes // 2) + 8, :]
        x = x if i < modes // 2 else pltpu.roll(x, modes, 1)
        parts.append(jnp.where(lane < modes, x, jnp.where(lane == row + (i + modes), 1.0, 0.0)))
    pivots = []
    for k in range(0, modes, STEP):
        g, r = k // 8, k % 8
        steps = range(STEP)
        rows = [parts[g][r + i : r + i + 1, :] for i in steps]
        block = [[jnp.broadcast_to(x[:, k + i : k + i + 1], x.shape) for i in steps] for x in rows]
        inverses = []
        for i in steps:
            inverses.append(1.0 / block[i][i])
            for j in range(i + 1, STEP):
                ratio = block[j][i] * inverses[i]
                block[j] = [x - ratio * y for x, y in zip(block[j], block[i])]
                rows[j] = rows[j] - ratio * rows[i]
            pivots.append(block[i][i])
        scaled = [x * inverse for x, inverse in zip(rows, inverses)]
        for n in range(g, modes // 8):
            part = parts[n]
            columns = [jnp.broadcast_to(part[:, k + i : k + i + 1], part.shape) for i in steps]
            for i in steps:
                for j in range(i + 1, STEP):
                    columns[j] = columns[j] - columns[i] * (block[i][j] * inverses[i])
            for i in steps:
                column = jnp.where(row >= r + STEP, columns[i], 0.0) if n == g else columns[i]
                part = part - column * scaled[i]
            if n == g:
                for i in steps:
                    part = jnp.where(row == r + i, rows[i], part)
            parts[n] = part
    for i in range(modes // 8):
        scale = 1.0 / jnp.sqrt(jnp.concatenate(pivots[i * 8 : (i + 1) * 8], axis=0))
        part = parts[i] * scale
        upper = jnp.where(lane >= row + i * 8, part / norm, 0.0)
        factor_ref[i * 8 : (i + 1) * 8, :] = upper[:, :modes]
        part = part * norm
        inverse_ref[i * 8 : (i + 1) * 8, :] = jnp.where(lane < modes, pltpu.roll(part, modes, 1), part)
    lhs = jnp.concatenate(split2(inverse_ref[...]), axis=0)
    copies = []
    for v in range(VARS):
        both = dot(lhs, field_ref[2 * v * modes : (2 * v + 2) * modes, :])
        held_ref[v] = both[:modes] + both[modes:]
        copies.append(pltpu.make_async_copy(held_ref.at[v], out_ref.at[v], done_ref.at[v]))
        copies[-1].start()
    for copy in copies:
        copy.wait()


def local(mode_shapes, wall_coupling, owner_dev, owner_cell, neighbours, coupling_blocks, inv_blocks):
    devices = lax.axis_size("slab")
    cells = inv_blocks.shape[2]
    nodes, modes = mode_shapes.shape[0], mode_shapes.shape[1] // 3
    cap = max(2, 2 * nodes // devices)
    rim = cells // 8
    groups = 128 // cap
    columns = 3 * modes + 3 * VARS + 1
    rows = round_up(-(-columns // groups), 8)
    rows16 = round_up(rows, 16)
    packed = call(
        functools.partial(pack_body, cap, groups, rows),
        jax.ShapeDtypeStruct((devices * rows, 128), F32),
        mode_shapes.T, wall_coupling.T, owner_dev.T, owner_cell[None, :],
        grid=(1,),
        in_specs=[pl.BlockSpec((n, nodes), lambda i: (0, 0)) for n in (3 * modes, 3 * VARS, 1, 1)],
        out_specs=pl.BlockSpec((devices * rows, 128), lambda i: (0, 0)),
        scratch=[pltpu.VMEM(((groups - 1) * rows + rows16, nodes), F32), pltpu.VMEM((groups, 2 * rows16, nodes), BF16)],
        name="pack", limit=60,
    )
    arrived = lax.all_to_all(packed, "slab", split_axis=0, concat_axis=0, tiled=True)
    field = jax.ShapeDtypeStruct((VARS, modes, cells), F32)
    field_two = jax.ShapeDtypeStruct((VARS * 2 * modes, cells), BF16)
    edge = jax.ShapeDtypeStruct((VARS, modes, rim), F32)
    blocks, place = call(
        functools.partial(prepare_body, rim),
        (jax.ShapeDtypeStruct((VARS * VARS * 8, cells), F32), jax.ShapeDtypeStruct((8, cells), I32)),
        (lax.axis_index("slab") * cells).astype(I32)[None], neighbours, coupling_blocks.transpose(1, 2, 0, 3), inv_blocks,
        in_specs=[pl.BlockSpec(memory_space=pltpu.SMEM)] + [VMEM] * 3,
        cost_estimate=pl.CostEstimate(flops=10**9, bytes_accessed=10**7, transcendentals=0),
        name="prepare",
    )
    start, two, first, final = call(
        functools.partial(forcing_body, cap, groups, rows, modes, rim),
        (field, field_two, edge, edge),
        arrived, inv_blocks,
        scratch=[
            pltpu.VMEM((groups * rows, devices * cap), F32),
            pltpu.VMEM((VARS * 2 * modes, devices * cap), BF16),
            pltpu.VMEM((devices * cap, 128), F32),
        ],
        name="forcing",
    )
    up = [(i, i + 1) for i in range(devices - 1)]
    down = [(j, i) for i, j in up]
    x = start
    inner = cells - 2 * rim
    mid = jax.ShapeDtypeStruct((VARS, modes, inner), F32)
    mid_two = jax.ShapeDtypeStruct((VARS * 2 * modes, inner), BF16)
    fetched = [
        pltpu.VMEM((VARS * 2 * modes, (NBR - BY_LANES) * 256), F32), pltpu.VMEM((2, VARS, modes, 128), F32)
    ]
    cost = pl.CostEstimate(flops=10**10, bytes_accessed=3 * 10**7, transcendentals=0)
    for last in (False, True):
        pairs = [(i, i ^ 1) for i in range(devices)]
        shifted = [(i, i + 1) for i in range(1, devices - 1, 2)]
        shifted = shifted + [(j, i) for i, j in shifted]
        even = lax.axis_index("slab") % 2 == 0
        one = lax.ppermute(jnp.where(even, final, first), "slab", pairs)
        other = lax.ppermute(jnp.where(even, first, final), "slab", shifted)
        before, after = jnp.where(even, other, one), jnp.where(even, one, other)
        middle = call(
            functools.partial(inner_body, rim, last), (mid_two,) if last else (mid, mid_two),
            x, two, start, place, blocks, scratch=fetched, cost_estimate=cost, name="inner_last" if last else "inner",
        )
        windows = [
            pltpu.VMEM((2, VARS, modes, 256 + 2 * rim), F32), pltpu.VMEM((2, VARS * 2 * modes, 256 + 2 * rim), BF16)
        ]
        if last:
            two, gram = call(
                functools.partial(outer_body, rim, last), (field_two, jax.ShapeDtypeStruct((modes // 2, 2 * modes), F32)),
                x, two, before, after, start, place, blocks, *middle,
                scratch=windows + fetched, name="outer_last",
            )
        else:
            x, two, first, final = call(
                functools.partial(outer_body, rim, last), (field, field_two, edge, edge),
                x, two, before, after, start, place, blocks, *middle, scratch=windows + fetched, name="outer",
            )
    reach = 1
    while reach < devices:
        gram = gram + lax.ppermute(gram, "slab", [(i, i ^ reach) for i in range(devices)])
        reach *= 2
    norm = math.sqrt(VARS * cells * devices)
    return call(
        functools.partial(basis_body, norm),
        (jax.ShapeDtypeStruct((VARS, modes, cells), F32), jax.ShapeDtypeStruct((modes, modes), F32)),
        gram, two,
        out_specs=(pl.BlockSpec(memory_space=pl.ANY), VMEM),
        scratch=[
            pltpu.VMEM((modes, 2 * modes), F32), pltpu.VMEM((VARS, modes, cells), F32), pltpu.SemaphoreType.DMA((VARS,))
        ],
        name="basis",
    )


def solution(mesh):
    in_specs = (
        P(("groups", "slab"), None),
        P(("groups", "slab"), None),
        P(("groups", "slab"), None),
        P(("groups", "slab")),
        P(None, ("groups", "slab")),
        P(None, None, None, ("groups", "slab")),
        P(None, None, ("groups", "slab")),
    )
    out_specs = (P(None, None, ("groups", "slab")), P("groups", None))
    return jax.shard_map(local, mesh=mesh, in_specs=in_specs, out_specs=out_specs, check_vma=False)
```
